512 devices in a mesh: sub: 8 (over y, core), front: 64 (over x, z).
Axes of the slice: x: 4, y: 4, z: 16, core: 2. Of those that a mesh axis runs over, the one named last changes fastest.
Arguments:
- rhs_root: float32 [22528, 128], P(('sub', 'front')), may hold values from -6 to 6
- rhs_level: float32 [11264, 128], P(('sub', 'front')), may hold values from -6 to 6
- root_inverse: bfloat16 [22528, 22528], P('front', 'sub'), as said below
- level_inverse: bfloat16 [11264, 11264], P('front', 'sub'), as said below
- coupling_t: bfloat16 [11264, 11264], P('front', 'sub'), may hold values from -0.078125 to 0.078125
- coupling_rows: int32 [64, 88], P('front', 'sub'), may hold values from 0 to 175, as said below
Outputs:
- root_potential: float32 [22528, 128], P(('sub', 'front'))
- level_potential: float32 [11264, 128], P(('sub', 'front'))
The draws below stay inside these ranges and needn't reach their ends.
Inputs may be any that keep to these rules, and one draw needn't show every extreme that they name: `root_inverse`: zero above the diagonal; diagonal entries between 0.5 and 1.5. `level_inverse`: zero above the diagonal; diagonal entries between 0.5 and 1.5. `coupling_rows`: entry [p, j] lies in the range of 22 blocks that starts at block (j // 11) * 22; the 11 entries of one panel in one range are distinct; every row block is named by some panel.
All inputs are finite; a program needn't handle non-finite values.
Results may differ from the reference program's by a relative error of at most 0.02.
Values may be sent and summed in bfloat16 or wider, within the bound.
A program may use at most 64 MiB of HBM per device.

```python
import math
import jax
import jax.numpy as jnp
from jax import lax

W0 = 22528
W1 = 11264
NRHS = 128
RB = 128
KEEP = 11
PANELS = 64
PANEL = 176
SLOTS = 88
ROW_BLOCKS = 176
BPS = 22


def lower_inverse(key, order, marker):
    entries = jax.random.normal(jax.random.fold_in(key, marker), (order, order), jnp.float32)
    diagonal = jax.random.uniform(jax.random.fold_in(key, marker + 1), (order,), jnp.float32, 0.5, 1.5)
    row_index = lax.broadcasted_iota(jnp.int32, (order, order), 0)
    col_index = lax.broadcasted_iota(jnp.int32, (order, order), 1)
    below = jnp.where(row_index > col_index, entries * (1.0 / math.sqrt(order)), 0.0)
    return jnp.where(row_index == col_index, diagonal[None, :], below).astype(jnp.bfloat16)


def draw_root_inverse(key, part):
    return lower_inverse(key, W0, 101)


def draw_level_inverse(key, part):
    return lower_inverse(key, W1, 203)


def draw_coupling_rows(key, part):
    groups = SLOTS // KEEP
    first_count = (BPS + PANELS - 1) // PANELS
    base_scores = jax.random.randint(jax.random.fold_in(key, 307), (groups, BPS), 0, 1 << 20)
    base_scores = base_scores * BPS + lax.broadcasted_iota(jnp.int32, (groups, BPS), 1)
    orders = jnp.argsort(base_scores, axis=1).astype(jnp.int32)
    ranks = jnp.argsort(orders, axis=1).astype(jnp.int32)
    panel_index = lax.broadcasted_iota(jnp.int32, (groups, PANELS, BPS), 1)
    forced = (ranks[:, None, :] - panel_index * first_count) % BPS < first_count
    panel_scores = jax.random.randint(jax.random.fold_in(key, 311), (groups, PANELS, BPS), 0, 1 << 20)
    panel_scores = panel_scores * BPS + lax.broadcasted_iota(jnp.int32, (groups, PANELS, BPS), 2)
    panel_scores = jnp.where(forced, panel_scores, panel_scores + (1 << 20) * BPS)
    chosen = jnp.argsort(panel_scores, axis=2)[:, :, :KEEP].astype(jnp.int32)
    chosen = chosen + lax.broadcasted_iota(jnp.int32, (groups, PANELS, KEEP), 0) * BPS
    return jnp.transpose(chosen, (1, 0, 2)).reshape(PANELS, SLOTS).astype(jnp.int32)


def steps_of(stream_key, shape, split, least, largest):
    gain = 1.0
    for dim, shards_of in split:
        steps = jax.random.uniform(jax.random.fold_in(jax.random.fold_in(stream_key, 6), dim), (shards_of,), jnp.float32, least / len(split), largest / len(split))
        gain = gain * jnp.repeat(jnp.exp(steps), shape[dim] // shards_of).reshape((-1,) + (1,) * (len(shape) - 1 - dim))
    return gain


def normal_values(key, shape, deviation, most, split=(), kind=jnp.bfloat16):
    level = steps_of(key, shape, split, -0.22, 0.18) if split else 1.0
    result = jax.random.normal(key, shape, jnp.float32) * deviation * level
    return jnp.minimum(jnp.maximum(result, -most), most).astype(kind)


def setup_inputs(seed: int = 0) -> dict:
    key_list = jax.random.split(jax.random.key(seed), 7)
    rhs_root = normal_values(key_list[0], (W0, NRHS), 1.0, 6.0, ((0, 512),), jnp.float32)
    rhs_level = normal_values(key_list[1], (W1, NRHS), 1.0, 6.0, ((0, 512),), jnp.float32)
    root_inverse = draw_root_inverse(jax.random.fold_in(key_list[6], 71), 0)
    level_inverse = draw_level_inverse(jax.random.fold_in(key_list[6], 71), 0)
    coupling_t = normal_values(key_list[4], (W1, SLOTS * RB), (W1 // 2) ** -0.5, 0.078125, ((0, 64), (1, 8)))
    coupling_rows = draw_coupling_rows(jax.random.fold_in(key_list[6], 71), 0)
    return dict(rhs_root=rhs_root, rhs_level=rhs_level, root_inverse=root_inverse, level_inverse=level_inverse, coupling_t=coupling_t, coupling_rows=coupling_rows)


def reference(rhs_root, rhs_level, root_inverse, level_inverse, coupling_t, coupling_rows):
    highest = lax.Precision.HIGHEST
    forward_level = jnp.dot(level_inverse, rhs_level.astype(jnp.bfloat16), preferred_element_type=jnp.float32)
    forward_level_b = forward_level.astype(jnp.bfloat16)
    blocks = coupling_t.reshape(PANELS, PANEL, SLOTS, RB).astype(jnp.float32)
    level_panels = forward_level_b.reshape(PANELS, PANEL, NRHS).astype(jnp.float32)
    pushed = jnp.einsum("pcsi,pcn->psin", blocks, level_panels, precision=highest)
    selector = (coupling_rows[:, :, None] == jnp.arange(ROW_BLOCKS, dtype=jnp.int32)[None, None, :]).astype(jnp.float32)
    update = jnp.einsum("psb,psin->bin", selector, pushed, precision=highest).reshape(W0, NRHS)
    shifted_b = (rhs_root - update).astype(jnp.bfloat16)
    forward_root = jnp.dot(root_inverse, shifted_b, preferred_element_type=jnp.float32)
    forward_root_b = forward_root.astype(jnp.bfloat16)
    root_potential = jnp.dot(root_inverse.T, forward_root_b, preferred_element_type=jnp.float32)
    root_potential_b = root_potential.astype(jnp.bfloat16)
    picked = root_potential_b.reshape(ROW_BLOCKS, RB, NRHS)[coupling_rows].astype(jnp.float32)
    pulled = jnp.einsum("pcsi,psin->pcn", blocks, picked, precision=highest).reshape(W1, NRHS)
    corrected_b = (forward_level - pulled).astype(jnp.bfloat16)
    level_potential = jnp.dot(level_inverse.T, corrected_b, preferred_element_type=jnp.float32)
    return (root_potential, level_potential)
```

```python
import jax
import jax.numpy as jnp
from jax import lax
from jax.experimental import pallas as pl
from jax.experimental.pallas import tpu as pltpu
from jax.sharding import PartitionSpec as P

RB = 128
NX, NZ, NY = 4, 16, 4
NF, NS = NX * NZ, NY * 2
CH = 176
F32, BF16 = jnp.float32, jnp.bfloat16


def rcopy(src, dst, ssem, rsem, dev):
    return pltpu.make_async_remote_copy(
        src_ref=src, dst_ref=dst, send_sem=ssem, recv_sem=rsem,
        device_id=dev, device_id_type=pl.DeviceIdType.MESH,
    )


def loop(n, fn):
    def step(i, carry):
        fn(i)
        return carry

    lax.fori_loop(0, n, step, 0)


def offset(k):
    half = (k + 1) // 2
    return NZ // 2 + half * (1 - 2 * (k % 2))


def tdot(a, b):
    return lax.dot_general(a, b, (((0,), (0,)), ((), ())), preferred_element_type=F32)


def kernel(
    rr, rl, l0_h, l1_h, ct_h, rows, rp_out, lp_out,
    l0, l1, ct, cs, cols, u, acc, own, stage, part, fl,
    ag1, ag2, ag3, ub1, ub2, ub3, xr1, xr2, xr3, zs1, zs2, zs3, zr1, zr2, zr3,
    sa1, sa2, sa3, sb1, sb2, sb3, sc1, sc2, sc3,
    ld, ag_s, ag_z, ag_x, rs_s, rs_x, rs_z, sub_s, sub_r,
):
    s, f = lax.axis_index("sub"), lax.axis_index("front")
    x, z, y, c = f // NZ, f % NZ, s // 2, s % 2

    def zdev(z2):
        return (s, x * NZ + z2)

    def xdev(e):
        return (s, ((x + e) % NX) * NZ + z)

    barrier = pltpu.get_barrier_semaphore()

    def greet(dev):
        pl.semaphore_signal(barrier, inc=1, device_id=dev, device_id_type=pl.DeviceIdType.MESH)

    loop(NZ - 1, lambda k: greet(zdev((z + offset(k)) % NZ)))
    for e in (2, 1, 3):
        greet(xdev(e))
    loop(NS - 1, lambda k: greet(((s + k + 1) % NS, f)))

    loads = [
        pltpu.make_async_copy(l1_h, l1, ld.at[0]),
        pltpu.make_async_copy(l0_h, l0, ld.at[1]),
    ]
    slots = ct.shape[0]
    for j in range(slots):
        loads.append(pltpu.make_async_copy(ct_h.at[:, j * RB:(j + 1) * RB], ct.at[j], ld.at[2 + j]))
    for load in loads:
        load.start()

    n1, n0 = rl.shape[0], rr.shape[0]
    p1, p0 = ag1.shape[1], ag2.shape[1]
    blocks = l0.shape[1] // RB

    stage[...] = jnp.zeros_like(stage)
    acc[...] = jnp.zeros_like(acc)
    part[...] = jnp.zeros_like(part)
    stage[0:n1, :] = rl[...]
    ag1[f] = stage[0:p1, :].astype(BF16)

    for load in loads:
        load.wait()
    ids = [lax.rem(rows[0, j], blocks) for j in range(slots)]
    for b in range(blocks):
        k, hit = jnp.int32(0), jnp.int32(0)
        for j in range(slots):
            same = ids[j] == b
            k = jnp.where(same, j, k)
            hit = jnp.where(same, 1, hit)
        cs[:, b * RB:(b + 1) * RB] = (ct[k].astype(F32) * hit.astype(F32)).astype(BF16)

    pl.semaphore_wait(barrier, NZ - 1 + NX - 1 + NS - 1)

    def gather(i, buf):
        def send(k):
            rcopy(buf.at[f], buf.at[f], ag_s.at[i], ag_z.at[i, z], zdev((z + offset(k)) % NZ)).start()

        loop(NZ - 1, send)

        def forward(slot):
            for e in (2, 1, 3):
                rcopy(buf.at[slot], buf.at[slot], ag_s.at[i], ag_x.at[i, e - 1], xdev(e)).start()

        forward(f)

        def relay(k):
            z2 = (z + NZ - offset(NZ - 2 - k)) % NZ
            slot = x * NZ + z2
            rcopy(buf.at[slot], buf.at[slot], ag_s.at[i], ag_z.at[i, z2], zdev(z2)).wait_recv()
            forward(slot)

        loop(NZ - 1, relay)
        for e in (1, 3, 2):
            got = buf.at[pl.ds(((x + NX - e) % NX) * NZ, NZ)]
            rcopy(got, got, ag_s.at[i], ag_x.at[i, e - 1], xdev(e)).wait_recv()

    def gather_done(i, buf):
        sent = buf.at[pl.ds(0, NF - 1)]
        rcopy(sent, sent, ag_s.at[i], ag_x.at[i, 0], xdev(1)).wait_send()

    def compact(buf, n):
        q = 88 // n

        def put(i):
            pieces = [buf[i * q + j].astype(F32)[:n] for j in range(q)]
            cols[pl.ds(pl.multiple_of(i * 88, 8), 88), :] = jnp.concatenate(pieces, axis=0)

        loop(NF // q, put)

    def scatter(i, n, pad, ub, xr, zs, zr):
        nc = ub.shape[0] // NX
        g = CH // n

        def cast(k):
            ub[k] = u[pl.ds(pl.multiple_of(k * CH, 8), CH), :].astype(BF16)

        loop(NX * nc, cast)
        far = ((z + NZ // 2) % NZ) // g
        order = [(far + d) % nc for d in ((0, 1, 3, 2) if nc == 4 else (0, 1))]
        for t in order:
            for e in (2, 1, 3):
                rcopy(
                    ub.at[((x + e) % NX) * nc + t], xr.at[e - 1, t], rs_s.at[i, 0],
                    rs_x.at[i, (e - 1) * nc + t], xdev(e),
                ).start()
        for t in order:
            for e in (1, 3, 2):
                rcopy(
                    ub.at[x * nc + t], xr.at[e - 1, t], rs_s.at[i, 0],
                    rs_x.at[i, (e - 1) * nc + t], xdev(e),
                ).wait_recv()
            total = u[pl.ds(pl.multiple_of((x * nc + t) * CH, 8), CH), :]
            for e in (1, 3, 2):
                total = total + xr[e - 1, t].astype(F32)
            acc[0:CH, :] = total
            for j in range(g):
                z2 = t * g + j
                piece = acc[j * n:j * n + pad, :]
                zs[z2] = piece.astype(BF16)

                @pl.when(z2 == z)
                def _():
                    own[0:pad, :] = piece

                @pl.when(z2 != z)
                def _():
                    rcopy(zs.at[z2], zr.at[z], rs_s.at[i, 1], rs_z.at[i, z], zdev(z2)).start()

        def add(k):
            z2 = (z + NZ - offset(NZ - 2 - k)) % NZ
            rcopy(zs.at[z2], zr.at[z2], rs_s.at[i, 1], rs_z.at[i, z2], zdev(z2)).wait_recv()
            own[0:pad, :] = own[0:pad, :] + zr[z2].astype(F32)

        loop(NZ - 1, add)

    def scatter_done(i, ub, zs):
        nc = ub.shape[0] // NX
        sent = ub.at[pl.ds(0, (NX - 1) * nc)]
        rcopy(sent, sent, rs_s.at[i, 0], rs_x.at[i, 0], xdev(1)).wait_send()
        sent = zs.at[pl.ds(0, NZ - 1)]
        rcopy(sent, sent, rs_s.at[i, 1], rs_z.at[i, 0], xdev(1)).wait_send()

    def sub_sum(i, a, b, d):
        h = a.shape[0]
        a[...] = part[pl.ds(pl.multiple_of((1 - c) * h, 8), h), :].astype(BF16)
        first = rcopy(a, b, sub_s.at[i, 0], sub_r.at[i, 0], (s + 1 - 2 * c, f))
        first.start()
        first.wait_recv()
        mine = part[pl.ds(pl.multiple_of(c * h, 8), h), :] + b[...].astype(F32)
        d[s] = mine.astype(BF16)

        def send(k):
            rcopy(d.at[s], d.at[s], sub_s.at[i, 1], sub_r.at[i, 1], ((s + k + 1) % NS, f)).start()

        loop(NS - 1, send)
        others = d.at[pl.ds(0, NS - 1)]
        rcopy(others, others, sub_s.at[i, 1], sub_r.at[i, 1], xdev(1)).wait_recv()
        halves = []
        for core in range(2):
            total = d[core].astype(F32)
            for k in range(1, NY):
                total = total + d[2 * k + core].astype(F32)
            halves.append(total)
        return halves

    def sub_done(i, a, b, d):
        rcopy(a, b, sub_s.at[i, 0], sub_r.at[i, 0], xdev(1)).wait_send()
        others = d.at[pl.ds(0, NS - 1)]
        rcopy(others, others, sub_s.at[i, 1], sub_r.at[i, 1], xdev(1)).wait_send()

    w1, w0 = l1.shape[0], l0.shape[0]
    k1, k0 = l1.shape[1], l0.shape[1]

    gather(0, ag1)
    compact(ag1, n1)
    part[0:w1, :] = jnp.dot(l1[...], cols[0:k1, :].astype(BF16), preferred_element_type=F32)
    top, bottom = sub_sum(0, sa1, sb1, sc1)
    h1 = sa1.shape[0]
    fl[0:h1, :] = top
    fl[h1:2 * h1, :] = bottom

    flb = fl[0:w1, :].astype(BF16)

    def push(b):
        at = pl.multiple_of(b * RB, RB)
        u[pl.ds(at, RB), :] = tdot(cs[:, pl.ds(at, RB)], flb)

    loop(blocks, push)
    scatter(0, n0, p0, ub1, xr1, zs1, zr1)
    stage[0:n0, :] = rr[...] - own[0:n0, :]
    ag2[f] = stage[0:p0, :].astype(BF16)

    gather(1, ag2)
    compact(ag2, n0)
    part[0:w0, :] = jnp.dot(l0[...], cols[...].astype(BF16), preferred_element_type=F32)
    top, bottom = sub_sum(1, sa2, sb2, sc2)
    h0 = sa2.shape[0]
    part[0:h0, :] = top
    part[h0:2 * h0, :] = bottom
    frb = part[0:w0, :].astype(BF16)

    def back(b):
        at = pl.multiple_of(b * RB, RB)
        u[pl.ds(at, RB), :] = tdot(l0[:, pl.ds(at, RB)], frb)

    loop(blocks, back)
    scatter(1, n0, p0, ub2, xr2, zs2, zr2)
    rp_out[...] = own[0:n0, :]
    ag3[f] = own[0:p0, :].astype(BF16)

    gather(2, ag3)
    compact(ag3, n0)
    part[w1:w0, :] = jnp.zeros((w0 - w1, part.shape[1]), F32)
    part[0:w1, :] = jnp.dot(cs[...], cols[...].astype(BF16), preferred_element_type=F32)
    top, bottom = sub_sum(2, sa3, sb3, sc3)
    fl[0:h1, :] = fl[0:h1, :] - top
    fl[h1:2 * h1, :] = fl[h1:2 * h1, :] - bottom
    corb = fl[0:w1, :].astype(BF16)

    def back_level(b):
        at = pl.multiple_of(b * RB, RB)
        u[pl.ds(at, RB), :] = tdot(l1[:, pl.ds(at, RB)], corb)

    loop(k1 // RB, back_level)
    scatter(2, n1, p1, ub3, xr3, zs3, zr3)
    lp_out[...] = own[0:n1, :]

    for i, buf in enumerate((ag1, ag2, ag3)):
        gather_done(i, buf)
    for i, (ub, zs) in enumerate(((ub1, zs1), (ub2, zs2), (ub3, zs3))):
        scatter_done(i, ub, zs)
    for i, (a, b, d) in enumerate(((sa1, sb1, sc1), (sa2, sb2, sc2), (sa3, sb3, sc3))):
        sub_done(i, a, b, d)


def body(rr, rl, l0, l1, ct, rows):
    w = rr.shape[1]
    n0, n1 = rr.shape[0], rl.shape[0]
    p0, p1 = 48, 32
    c0, c1 = CH // n0, CH // n1
    h0, h1 = l0.shape[0] // 2, 96
    vmem = pl.BlockSpec(memory_space=pltpu.VMEM)
    hbm = pl.BlockSpec(memory_space=pl.ANY)
    slots = ct.shape[1] // RB
    scratch = [
        pltpu.VMEM(l0.shape, BF16), pltpu.VMEM(l1.shape, BF16), pltpu.VMEM((slots, ct.shape[0], RB), BF16),
        pltpu.VMEM((ct.shape[0], l0.shape[1]), BF16), pltpu.VMEM((l0.shape[1], w), F32),
        pltpu.VMEM((l0.shape[1], w), F32), pltpu.VMEM((192, w), F32), pltpu.VMEM((p0, w), F32),
        pltpu.VMEM((p0, w), F32), pltpu.VMEM((l0.shape[0], w), F32), pltpu.VMEM((2 * h1, w), F32),
    ]
    pads, chunks, halves = (p0, p0, p1), (NZ // c0, NZ // c0, NZ // c1), (h1, h0, h1)
    scratch += [pltpu.VMEM((NF, p, w), BF16) for p in (p1, p0, p0)]
    scratch += [pltpu.VMEM((NX * k, CH, w), BF16) for k in chunks]
    scratch += [pltpu.VMEM((NX - 1, k, CH, w), BF16) for k in chunks]
    scratch += [pltpu.VMEM((NZ, p, w), BF16) for p in pads]
    scratch += [pltpu.VMEM((NZ, p, w), BF16) for p in pads]
    scratch += [pltpu.VMEM((h, w), BF16) for h in halves]
    scratch += [pltpu.VMEM((h, w), BF16) for h in halves]
    scratch += [pltpu.VMEM((NS, h, w), BF16) for h in halves]
    dma = pltpu.SemaphoreType.DMA
    scratch += [
        dma((2 + slots,)), dma((3,)), dma((3, NZ)), dma((3, NX - 1)), dma((3, 2)), dma((3, (NX - 1) * max(chunks))),
        dma((3, NZ)), dma((3, 2)), dma((3, 2)),
    ]
    return pl.pallas_call(
        kernel,
        out_shape=(jax.ShapeDtypeStruct((n0, w), F32), jax.ShapeDtypeStruct((n1, w), F32)),
        in_specs=[vmem, vmem, hbm, hbm, hbm, pl.BlockSpec(memory_space=pltpu.SMEM)],
        out_specs=(vmem, vmem),
        scratch_shapes=scratch,
        compiler_params=pltpu.CompilerParams(
            collective_id=0, has_side_effects=True, vmem_limit_bytes=40 << 20
        ),
    )(rr, rl, l0, l1, ct, rows)


def solution(mesh):
    return jax.shard_map(
        body,
        mesh=mesh,
        in_specs=(
            P(("sub", "front"), None),
            P(("sub", "front"), None),
            P("front", "sub"),
            P("front", "sub"),
            P("front", "sub"),
            P("front", "sub"),
        ),
        out_specs=(P(("sub", "front"), None), P(("sub", "front"), None)),
        check_vma=False,
    )
```

```python
import jax
import jax.numpy as jnp
from jax import lax
from jax.experimental import pallas as pl
from jax.experimental.pallas import tpu as pltpu
from jax.sharding import PartitionSpec as P

RB = 128
NX, NZ, NY = 4, 16, 4
NF, NS = NX * NZ, NY * 2
CH = 176
F32, BF16 = jnp.float32, jnp.bfloat16


def rcopy(src, dst, ssem, rsem, dev):
    return pltpu.make_async_remote_copy(
        src_ref=src, dst_ref=dst, send_sem=ssem, recv_sem=rsem,
        device_id=dev, device_id_type=pl.DeviceIdType.MESH,
    )


def loop(n, fn):
    def step(i, carry):
        fn(i)
        return carry

    lax.fori_loop(0, n, step, 0)


def offset(k):
    half = (k + 1) // 2
    return NZ // 2 + half * (1 - 2 * (k % 2))


def kernel(
    rr_h, rl_h, l0_h, l1_h, ct_h, rows, rp_out, lp_out,
    rr, rl, l0, l0t, l1, l1t, ct, cs, cst, cols, u, acc, own, stage, part, fl,
    ag1, ag2, ag3, ub1, ub2, ub3, xr1, xr2, xr3, zs1, zs2, zs3, zr1, zr2, zr3,
    sa1, sa2, sa3, sb1, sb2, sb3, sc1, sc2, sc3,
    ld, ag_s, ag_z, ag_x, rs_s, rs_x, rs_z, sub_s, sub_r,
):
    s, f = lax.axis_index("sub"), lax.axis_index("front")
    x, z, y, c = f // NZ, f % NZ, s // 2, s % 2

    def zdev(z2):
        return (s, x * NZ + z2)

    def xdev(e):
        return (s, ((x + e) % NX) * NZ + z)

    pending = []
    barrier = pltpu.get_barrier_semaphore()

    def greet(dev):
        pl.semaphore_signal(barrier, inc=1, device_id=dev, device_id_type=pl.DeviceIdType.MESH)

    loop(NZ - 1, lambda k: greet(zdev((z + offset(k)) % NZ)))
    for e in (2, 1, 3):
        greet(xdev(e))
    loop(NS - 1, lambda k: greet(((s + k + 1) % NS, f)))

    loads = [
        pltpu.make_async_copy(rl_h, rl, ld.at[0]),
        pltpu.make_async_copy(l1_h, l1, ld.at[1]),
        pltpu.make_async_copy(l0_h, l0, ld.at[2]),
        pltpu.make_async_copy(rr_h, rr, ld.at[3]),
    ]
    slots = ct.shape[0]
    for j in range(slots):
        loads.append(pltpu.make_async_copy(ct_h.at[:, j * RB:(j + 1) * RB], ct.at[j], ld.at[4 + j]))
    for load in loads:
        load.start()

    n1, n0 = rl.shape[0], rr.shape[0]
    p1, p0 = ag1.shape[1], ag2.shape[1]
    blocks = l0.shape[1] // RB

    stage[...] = jnp.zeros_like(stage)
    acc[...] = jnp.zeros_like(acc)
    part[...] = jnp.zeros_like(part)
    loads[0].wait()
    stage[0:n1, :] = rl[...]
    ag1[f] = stage[0:p1, :].astype(BF16)

    pl.semaphore_wait(barrier, NZ - 1 + NX - 1 + NS - 1)

    def gather(i, buf, n, meanwhile):
        pending.append(lambda: gather_done(i, buf))
        q = 88 // n

        def forward(slot):
            for e in (2, 1, 3):
                rcopy(buf.at[slot], buf.at[slot], ag_s.at[i], ag_x.at[i, e - 1], xdev(e)).start()

        def send(k):
            rcopy(buf.at[f], buf.at[f], ag_s.at[i], ag_z.at[i, z], zdev((z + offset(NZ - 2 - k)) % NZ)).start()

        def relay(k):
            z2 = (z + NZ - offset(NZ - 2 - k)) % NZ
            slot = x * NZ + z2
            rcopy(buf.at[slot], buf.at[slot], ag_s.at[i], ag_z.at[i, z2], zdev(z2)).wait_recv()
            forward(slot)

        def compact(quarter):
            def put(j):
                at = quarter * (NZ // q) + j
                pieces = [buf[at * q + m].astype(F32)[:n] for m in range(q)]
                cols[pl.ds(pl.multiple_of(at * 88, 8), 88), :] = jnp.concatenate(pieces, axis=0)

            loop(NZ // q, put)

        forward(f)
        loop(NZ - 1, send)
        meanwhile()
        loop(NZ - 1, relay)
        compact(x)
        for e in (1, 3, 2):
            quarter = (x + NX - e) % NX
            got = buf.at[pl.ds(quarter * NZ, NZ)]
            rcopy(got, got, ag_s.at[i], ag_x.at[i, e - 1], xdev(e)).wait_recv()
            compact(quarter)

    def gather_done(i, buf):
        sent = buf.at[pl.ds(0, NF - 1)]
        rcopy(sent, sent, ag_s.at[i], ag_x.at[i, 0], xdev(1)).wait_send()

    def scatter(i, n, pad, mat, vec, ub, xr, zs, zr):
        pending.append(lambda: scatter_done(i, ub, zs))
        nc = ub.shape[0] // NX
        g = CH // n

        def product(k):
            return jnp.dot(mat[pl.ds(pl.multiple_of(k * CH, 16), CH), :], vec, preferred_element_type=F32)

        far = ((z + NZ // 2) % NZ) // g
        order = [(far + d) % nc for d in ((0, 1, 3, 2) if nc == 4 else (0, 1))]
        for t in order:
            for e in (2, 1, 3):
                k = ((x + e) % NX) * nc + t
                ub[k] = product(k).astype(BF16)
                rcopy(
                    ub.at[k], xr.at[e - 1, t], rs_s.at[i, 0], rs_x.at[i, (e - 1) * nc + t], xdev(e),
                ).start()
        for t in order:
            u[t] = product(x * nc + t)
        for t in order:
            total = u[t]
            for e in (1, 3, 2):
                rcopy(
                    ub.at[t], xr.at[e - 1, t], rs_s.at[i, 0], rs_x.at[i, (e - 1) * nc + t], xdev(e),
                ).wait_recv()
                total = total + xr[e - 1, t].astype(F32)
            acc[0:CH, :] = total
            for j in range(g):
                z2 = t * g + j
                piece = acc[j * n:j * n + pad, :]
                zs[z2] = piece.astype(BF16)

                @pl.when(z2 == z)
                def _():
                    own[0:pad, :] = piece

                @pl.when(z2 != z)
                def _():
                    rcopy(zs.at[z2], zr.at[z], rs_s.at[i, 1], rs_z.at[i, z], zdev(z2)).start()

        def add(k):
            z2 = (z + NZ - offset(NZ - 2 - k)) % NZ
            rcopy(zs.at[z2], zr.at[z2], rs_s.at[i, 1], rs_z.at[i, z2], zdev(z2)).wait_recv()
            own[0:pad, :] = own[0:pad, :] + zr[z2].astype(F32)

        loop(NZ - 1, add)

    def scatter_done(i, ub, zs):
        nc = ub.shape[0] // NX
        sent = ub.at[pl.ds(0, (NX - 1) * nc)]
        rcopy(sent, sent, rs_s.at[i, 0], rs_x.at[i, 0], xdev(1)).wait_send()
        sent = zs.at[pl.ds(0, NZ - 1)]
        rcopy(sent, sent, rs_s.at[i, 1], rs_z.at[i, 0], xdev(1)).wait_send()

    def sub_sum(i, a, b, d, meanwhile):
        pending.append(lambda: sub_done(i, a, b, d))
        h = a.shape[0]
        a[...] = part[pl.ds(pl.multiple_of((1 - c) * h, 8), h), :].astype(BF16)
        first = rcopy(a, b, sub_s.at[i, 0], sub_r.at[i, 0], (s + 1 - 2 * c, f))
        first.start()
        first.wait_recv()
        mine = part[pl.ds(pl.multiple_of(c * h, 8), h), :] + b[...].astype(F32)
        d[s] = mine.astype(BF16)

        def send(k):
            rcopy(d.at[s], d.at[s], sub_s.at[i, 1], sub_r.at[i, 1], ((s + k + 1) % NS, f)).start()

        loop(NS - 1, send)
        meanwhile()
        others = d.at[pl.ds(0, NS - 1)]
        rcopy(others, others, sub_s.at[i, 1], sub_r.at[i, 1], xdev(1)).wait_recv()
        halves = []
        for core in range(2):
            total = d[core].astype(F32)
            for k in range(1, NY):
                total = total + d[2 * k + core].astype(F32)
            halves.append(total)
        return halves

    def sub_done(i, a, b, d):
        rcopy(a, b, sub_s.at[i, 0], sub_r.at[i, 0], xdev(1)).wait_send()
        others = d.at[pl.ds(0, NS - 1)]
        rcopy(others, others, sub_s.at[i, 1], sub_r.at[i, 1], xdev(1)).wait_send()

    w1, w0 = l1.shape[0], l0.shape[0]
    k1 = l1.shape[1]

    def transpose(mat, out):
        def put(k):
            at = pl.multiple_of(k * RB, RB)
            out[pl.ds(at, RB), :] = mat[:, pl.ds(at, RB)].T

        loop(mat.shape[1] // RB, put)

    def prepare():
        for load in loads[1:]:
            load.wait()
        ids = [lax.rem(rows[0, j], blocks) for j in range(slots)]
        for b in range(blocks):
            k, hit = jnp.int32(0), jnp.int32(0)
            for j in range(slots):
                same = ids[j] == b
                k = jnp.where(same, j, k)
                hit = jnp.where(same, 1, hit)
            cs[:, b * RB:(b + 1) * RB] = (ct[k].astype(F32) * hit.astype(F32)).astype(BF16)

    def nothing():
        pass

    gather(0, ag1, n1, prepare)
    part[0:w1, :] = jnp.dot(l1[...], cols[0:k1, :].astype(BF16), preferred_element_type=F32)
    top, bottom = sub_sum(0, sa1, sb1, sc1, lambda: transpose(cs, cst))
    h1 = sa1.shape[0]
    fl[0:h1, :] = top
    fl[h1:2 * h1, :] = bottom

    scatter(0, n0, p0, cst, fl[0:w1, :].astype(BF16), ub1, xr1, zs1, zr1)
    stage[0:n0, :] = rr[...] - own[0:n0, :]
    ag2[f] = stage[0:p0, :].astype(BF16)

    gather(1, ag2, n0, lambda: transpose(l0, l0t))
    part[0:w0, :] = jnp.dot(l0[...], cols[...].astype(BF16), preferred_element_type=F32)
    top, bottom = sub_sum(1, sa2, sb2, sc2, lambda: transpose(l1, l1t))
    h0 = sa2.shape[0]
    part[0:h0, :] = top
    part[h0:2 * h0, :] = bottom

    scatter(1, n0, p0, l0t, part[0:w0, :].astype(BF16), ub2, xr2, zs2, zr2)
    rp_out[...] = own[0:n0, :]
    ag3[f] = own[0:p0, :].astype(BF16)

    gather(2, ag3, n0, nothing)
    part[w1:w0, :] = jnp.zeros((w0 - w1, part.shape[1]), F32)
    part[0:w1, :] = jnp.dot(cs[...], cols[...].astype(BF16), preferred_element_type=F32)
    top, bottom = sub_sum(2, sa3, sb3, sc3, nothing)
    fl[0:h1, :] = fl[0:h1, :] - top
    fl[h1:2 * h1, :] = fl[h1:2 * h1, :] - bottom

    scatter(2, n1, p1, l1t, fl[0:w1, :].astype(BF16), ub3, xr3, zs3, zr3)
    lp_out[...] = own[0:n1, :]

    for fin in pending:
        fin()


def body(rr, rl, l0, l1, ct, rows):
    w = rr.shape[1]
    n0, n1 = rr.shape[0], rl.shape[0]
    p0, p1 = 48, 32
    c0, c1 = CH // n0, CH // n1
    h0, h1 = l0.shape[0] // 2, 96
    vmem = pl.BlockSpec(memory_space=pltpu.VMEM)
    hbm = pl.BlockSpec(memory_space=pl.ANY)
    slots = ct.shape[1] // RB
    scratch = [
        pltpu.VMEM(rr.shape, F32), pltpu.VMEM(rl.shape, F32),
        pltpu.VMEM(l0.shape, BF16), pltpu.VMEM(l0.shape[::-1], BF16),
        pltpu.VMEM(l1.shape, BF16), pltpu.VMEM(l1.shape[::-1], BF16), pltpu.VMEM((slots, ct.shape[0], RB), BF16),
        pltpu.VMEM((ct.shape[0], l0.shape[1]), BF16), pltpu.VMEM((l0.shape[1], ct.shape[0]), BF16),
        pltpu.VMEM((l0.shape[1], w), F32), pltpu.VMEM((NZ // min(c0, c1), CH, w), F32), pltpu.VMEM((192, w), F32), pltpu.VMEM((p0, w), F32),
        pltpu.VMEM((p0, w), F32), pltpu.VMEM((l0.shape[0], w), F32), pltpu.VMEM((2 * h1, w), F32),
    ]
    pads, chunks, halves = (p0, p0, p1), (NZ // c0, NZ // c0, NZ // c1), (h1, h0, h1)
    scratch += [pltpu.VMEM((NF, p, w), BF16) for p in (p1, p0, p0)]
    scratch += [pltpu.VMEM((NX * k, CH, w), BF16) for k in chunks]
    scratch += [pltpu.VMEM((NX - 1, k, CH, w), BF16) for k in chunks]
    scratch += [pltpu.VMEM((NZ, p, w), BF16) for p in pads]
    scratch += [pltpu.VMEM((NZ, p, w), BF16) for p in pads]
    scratch += [pltpu.VMEM((h, w), BF16) for h in halves]
    scratch += [pltpu.VMEM((h, w), BF16) for h in halves]
    scratch += [pltpu.VMEM((NS, h, w), BF16) for h in halves]
    dma = pltpu.SemaphoreType.DMA
    scratch += [
        dma((4 + slots,)), dma((3,)), dma((3, NZ)), dma((3, NX - 1)), dma((3, 2)), dma((3, (NX - 1) * max(chunks))),
        dma((3, NZ)), dma((3, 2)), dma((3, 2)),
    ]
    return pl.pallas_call(
        kernel,
        out_shape=(jax.ShapeDtypeStruct((n0, w), F32), jax.ShapeDtypeStruct((n1, w), F32)),
        in_specs=[hbm, hbm, hbm, hbm, hbm, pl.BlockSpec(memory_space=pltpu.SMEM)],
        out_specs=(vmem, vmem),
        scratch_shapes=scratch,
        compiler_params=pltpu.CompilerParams(
            collective_id=0, has_side_effects=True, vmem_limit_bytes=60 << 20
        ),
    )(rr, rl, l0, l1, ct, rows)


def solution(mesh):
    return jax.shard_map(
        body,
        mesh=mesh,
        in_specs=(
            P(("sub", "front"), None),
            P(("sub", "front"), None),
            P("front", "sub"),
            P("front", "sub"),
            P("front", "sub"),
            P("front", "sub"),
        ),
        out_specs=(P(("sub", "front"), None), P(("sub", "front"), None)),
        check_vma=False,
    )
```

```python
import jax
import jax.numpy as jnp
from jax import lax
from jax.experimental import pallas as pl
from jax.experimental.pallas import tpu as pltpu
from jax.sharding import PartitionSpec as P

RB = 128
NX, NZ, NY = 4, 16, 4
NF, NS = NX * NZ, NY * 2
CH = 176
F32, BF16 = jnp.float32, jnp.bfloat16


def rcopy(src, dst, ssem, rsem, dev):
    return pltpu.make_async_remote_copy(
        src_ref=src, dst_ref=dst, send_sem=ssem, recv_sem=rsem,
        device_id=dev, device_id_type=pl.DeviceIdType.MESH,
    )


def loop(n, fn):
    def step(i, carry):
        fn(i)
        return carry

    lax.fori_loop(0, n, step, 0)


def offset(k):
    half = (k + 1) // 2
    return NZ // 2 + half * (1 - 2 * (k % 2))


def kernel(
    rr_h, rl_h, l0_h, l1_h, ct_h, rows, rp_out, lp_out,
    rr, rl, l0, l0t, l1, l1t, ct, cs, cst, cols, u, acc, own, stage, part, fl,
    ag1, ag2, ag3, ub1, ub2, ub3, xr1, xr2, xr3, zs1, zs2, zs3, zr1, zr2, zr3,
    sd1, sd2, sd3, sa1, sa2, sa3, sa4, sb1, sb2, sb3, sb4,
    ld, ag_s, ag_z, ag_x, rs_s, rs_x, rs_z, sub_s, sub_r,
):
    s, f = lax.axis_index("sub"), lax.axis_index("front")
    x, z, y, c = f // NZ, f % NZ, s // 2, s % 2

    def zdev(z2):
        return (s, x * NZ + z2)

    def xdev(e):
        return (s, ((x + e) % NX) * NZ + z)

    pending = []
    barrier = pltpu.get_barrier_semaphore()

    def greet(dev):
        pl.semaphore_signal(barrier, inc=1, device_id=dev, device_id_type=pl.DeviceIdType.MESH)

    loop(NZ - 1, lambda k: greet(zdev((z + offset(k)) % NZ)))
    for e in (2, 1, 3):
        greet(xdev(e))
    for k in (2, 1, 3):
        greet((((y + k) % NY) * 2 + c, f))
    greet((s + 1 - 2 * c, f))

    loads = [
        pltpu.make_async_copy(rl_h, rl, ld.at[0]),
        pltpu.make_async_copy(l1_h, l1, ld.at[1]),
        pltpu.make_async_copy(l0_h, l0, ld.at[2]),
        pltpu.make_async_copy(rr_h, rr, ld.at[3]),
    ]
    slots = ct.shape[0]
    for j in range(slots):
        loads.append(pltpu.make_async_copy(ct_h.at[:, j * RB:(j + 1) * RB], ct.at[j], ld.at[4 + j]))
    for load in loads:
        load.start()

    n1, n0 = rl.shape[0], rr.shape[0]
    p1, p0 = ag1.shape[1], ag2.shape[1]
    blocks = l0.shape[1] // RB

    stage[...] = jnp.zeros_like(stage)
    acc[...] = jnp.zeros_like(acc)
    loads[0].wait()
    stage[0:n1, :] = rl[...]
    ag1[f] = stage[0:p1, :].astype(BF16)

    def prepare():
        for load in loads[1:]:
            load.wait()
        ids = [lax.rem(rows[0, j], blocks) for j in range(slots)]
        for b in range(blocks):
            k, hit = jnp.int32(0), jnp.int32(0)
            for j in range(slots):
                same = ids[j] == b
                k = jnp.where(same, j, k)
                hit = jnp.where(same, 1, hit)
            cs[:, b * RB:(b + 1) * RB] = (ct[k].astype(F32) * hit.astype(F32)).astype(BF16)

    prepare()
    pl.semaphore_wait(barrier, NZ - 1 + NX - 1 + NY)

    def gather(i, buf, n, meanwhile):
        pending.append(lambda: gather_done(i, buf))
        q = 88 // n

        def slot(d):
            return x * NZ + (z + d) % NZ

        def forward(d):
            for e in (2, 1, 3):
                rcopy(buf.at[slot(d)], buf.at[slot(d)], ag_s.at[i], ag_x.at[i, e - 1], xdev(e)).start()

        def send(d, to):
            rcopy(
                buf.at[slot(d)], buf.at[slot(d)], ag_s.at[i], ag_z.at[i, (z + d) % NZ], zdev((z + to) % NZ)
            ).start()

        def arrive(d):
            d = d % NZ
            rcopy(buf.at[slot(d)], buf.at[slot(d)], ag_s.at[i], ag_z.at[i, (z + d) % NZ], zdev((z + d) % NZ)).wait_recv()

        def compact(quarter):
            def put(j):
                at = quarter * (NZ // q) + j
                pieces = [buf[at * q + m].astype(F32)[:n] for m in range(q)]
                cols[pl.ds(pl.multiple_of(at * 88, 8), 88), :] = jnp.concatenate(pieces, axis=0)

            loop(NZ // q, put)

        forward(0)
        for to in (4, 12, 3, 13, 2, 14, 1, 15):
            send(0, to)
        meanwhile()
        for d in (1, 15, 2, 14):
            arrive(d)
            forward(d)
        for way in (NZ - 4, 4):
            arrive(way)

            @pl.when(z % 2 == (way == 4))
            def _():
                send(way, NZ - way)

            for m in (3, 2, 1):
                send(way, m if way == NZ - 4 else NZ - m)
        for d in (12, 4):
            forward(d)
        for d in (3, 13):
            arrive(d)
            forward(d)
        for d in (5, 11, 6, 10, 7, 9, 8):
            arrive(d)
            forward(d)
        compact(x)
        for e in (1, 3, 2):
            quarter = (x + NX - e) % NX
            got = buf.at[pl.ds(quarter * NZ, NZ)]
            rcopy(got, got, ag_s.at[i], ag_x.at[i, e - 1], xdev(e)).wait_recv()
            compact(quarter)

    def gather_done(i, buf):
        sent = buf.at[pl.ds(0, NF - 1)]
        rcopy(sent, sent, ag_s.at[i], ag_x.at[i, 0], xdev(1)).wait_send()

    def scatter(i, n, pad, mat, vec, ub, xr, zs, zr):
        pending.append(lambda: scatter_done(i, ub, zs))
        nc = ub.shape[0] // NX
        g = CH // n

        def product(k):
            return jnp.dot(mat[pl.ds(pl.multiple_of(k * CH, 16), CH), :], vec, preferred_element_type=F32)

        far = ((z + NZ // 2) % NZ) // g
        order = [(far + d) % nc for d in ((0, 1, 3, 2) if nc == 4 else (0, 1))]
        for t in order:
            for e in (2, 1, 3):
                k = ((x + e) % NX) * nc + t
                ub[k] = product(k).astype(BF16)
                rcopy(
                    ub.at[k], xr.at[e - 1, t], rs_s.at[i, 0], rs_x.at[i, (e - 1) * nc + t], xdev(e),
                ).start()
        for t in order:
            u[t] = product(x * nc + t)
        for t in order:
            total = u[t]
            for e in (1, 3, 2):
                rcopy(
                    ub.at[t], xr.at[e - 1, t], rs_s.at[i, 0], rs_x.at[i, (e - 1) * nc + t], xdev(e),
                ).wait_recv()
                total = total + xr[e - 1, t].astype(F32)
            acc[0:CH, :] = total
            for j in range(g):
                z2 = t * g + j
                piece = acc[j * n:j * n + pad, :]
                zs[z2] = piece.astype(BF16)

                @pl.when(z2 == z)
                def _():
                    own[0:pad, :] = piece

                @pl.when(z2 != z)
                def _():
                    rcopy(zs.at[z2], zr.at[z], rs_s.at[i, 1], rs_z.at[i, z], zdev(z2)).start()

        def add(k):
            z2 = (z + NZ - offset(NZ - 2 - k)) % NZ
            rcopy(zs.at[z2], zr.at[z2], rs_s.at[i, 1], rs_z.at[i, z2], zdev(z2)).wait_recv()
            own[0:pad, :] = own[0:pad, :] + zr[z2].astype(F32)

        loop(NZ - 1, add)

    def scatter_done(i, ub, zs):
        nc = ub.shape[0] // NX
        sent = ub.at[pl.ds(0, (NX - 1) * nc)]
        rcopy(sent, sent, rs_s.at[i, 0], rs_x.at[i, 0], xdev(1)).wait_send()
        sent = zs.at[pl.ds(0, NZ - 1)]
        rcopy(sent, sent, rs_s.at[i, 1], rs_z.at[i, 0], xdev(1)).wait_send()

    def swap(i, step, a, b):
        first = rcopy(a, b, sub_s.at[i, step], sub_r.at[i, step], (s + 1 - 2 * c, f))
        first.start()
        pending.append(first.wait_send)
        first.wait_recv()

    def sum_y(i, step, mine, d, meanwhile):
        d[y] = mine.astype(BF16)
        for k in (2, 1, 3):
            rcopy(
                d.at[y], d.at[y], sub_s.at[i, step], sub_r.at[i, step], (((y + k) % NY) * 2 + c, f)
            ).start()
        meanwhile()
        others = rcopy(
            d.at[pl.ds(0, NY - 1)], d.at[pl.ds(0, NY - 1)], sub_s.at[i, step], sub_r.at[i, step], xdev(1)
        )
        pending.append(others.wait_send)
        others.wait_recv()
        for k in range(1, NY):
            mine = mine + d[(y + k) % NY].astype(F32)
        return mine

    def sum_level(i, d, a, b, meanwhile):
        total = sum_y(i, 0, part[0:CH, :], d, meanwhile)
        a[...] = total.astype(BF16)
        swap(i, 1, a, b)
        return total + b[...].astype(F32)

    def sum_root(i, d, a, b, a2, b2, meanwhile):
        low, high = pl.multiple_of(c * CH, 8), pl.multiple_of((1 - c) * CH, 8)
        a[...] = part[pl.ds(high, CH), :].astype(BF16)
        swap(i, 0, a, b)
        total = sum_y(i, 1, part[pl.ds(low, CH), :] + b[...].astype(F32), d, meanwhile)
        a2[...] = total.astype(BF16)
        swap(i, 2, a2, b2)
        part[pl.ds(low, CH), :] = total
        part[pl.ds(high, CH), :] = b2[...].astype(F32)

    w1 = l1.shape[0]
    k1 = l1.shape[1]

    def transpose(mat, out):
        def put(k):
            at = pl.multiple_of(k * RB, RB)
            out[pl.ds(at, RB), :] = mat[:, pl.ds(at, RB)].T

        loop(mat.shape[1] // RB, put)

    def nothing():
        pass

    gather(0, ag1, n1, nothing)
    part[0:w1, :] = jnp.dot(l1[...], cols[0:k1, :].astype(BF16), preferred_element_type=F32)
    fl[...] = sum_level(0, sd1, sa1, sb1, lambda: transpose(cs, cst))

    scatter(0, n0, p0, cst, fl[...].astype(BF16), ub1, xr1, zs1, zr1)
    stage[0:n0, :] = rr[...] - own[0:n0, :]
    ag2[f] = stage[0:p0, :].astype(BF16)

    gather(1, ag2, n0, lambda: transpose(l0, l0t))
    part[...] = jnp.dot(l0[...], cols[...].astype(BF16), preferred_element_type=F32)
    sum_root(1, sd2, sa2, sb2, sa4, sb4, lambda: transpose(l1, l1t))

    scatter(1, n0, p0, l0t, part[...].astype(BF16), ub2, xr2, zs2, zr2)
    rp_out[...] = own[0:n0, :]
    ag3[f] = own[0:p0, :].astype(BF16)

    gather(2, ag3, n0, nothing)
    part[0:w1, :] = jnp.dot(cs[...], cols[...].astype(BF16), preferred_element_type=F32)
    fl[...] = fl[...] - sum_level(2, sd3, sa3, sb3, nothing)

    scatter(2, n1, p1, l1t, fl[...].astype(BF16), ub3, xr3, zs3, zr3)
    lp_out[...] = own[0:n1, :]

    for fin in pending:
        fin()


def hand_over(a, b, c, d):
    c[...] = a[...]
    d[...] = b[...]


def body(rr, rl, l0, l1, ct, rows):
    w = rr.shape[1]
    n0, n1 = rr.shape[0], rl.shape[0]
    p0, p1 = 48, 32
    c0, c1 = CH // n0, CH // n1
    vmem = pl.BlockSpec(memory_space=pltpu.VMEM)
    hbm = pl.BlockSpec(memory_space=pl.ANY)
    slots = ct.shape[1] // RB
    scratch = [
        pltpu.VMEM(rr.shape, F32), pltpu.VMEM(rl.shape, F32),
        pltpu.VMEM(l0.shape, BF16), pltpu.VMEM(l0.shape[::-1], BF16),
        pltpu.VMEM(l1.shape, BF16), pltpu.VMEM(l1.shape[::-1], BF16), pltpu.VMEM((slots, ct.shape[0], RB), BF16),
        pltpu.VMEM((ct.shape[0], l0.shape[1]), BF16), pltpu.VMEM((l0.shape[1], ct.shape[0]), BF16),
        pltpu.VMEM((l0.shape[1], w), F32), pltpu.VMEM((NZ // min(c0, c1), CH, w), F32), pltpu.VMEM((192, w), F32), pltpu.VMEM((p0, w), F32),
        pltpu.VMEM((p0, w), F32), pltpu.VMEM((l0.shape[0], w), F32), pltpu.VMEM((l1.shape[0], w), F32),
    ]
    pads, chunks = (p0, p0, p1), (NZ // c0, NZ // c0, NZ // c1)
    scratch += [pltpu.VMEM((NF, p, w), BF16) for p in (p1, p0, p0)]
    scratch += [pltpu.VMEM((NX * k, CH, w), BF16) for k in chunks]
    scratch += [pltpu.VMEM((NX - 1, k, CH, w), BF16) for k in chunks]
    scratch += [pltpu.VMEM((NZ, p, w), BF16) for p in pads]
    scratch += [pltpu.VMEM((NZ, p, w), BF16) for p in pads]
    scratch += [pltpu.VMEM((NY, CH, w), BF16) for _ in range(3)]
    scratch += [pltpu.VMEM((CH, w), BF16) for _ in range(8)]
    dma = pltpu.SemaphoreType.DMA
    scratch += [
        dma((4 + slots,)), dma((3,)), dma((3, NZ)), dma((3, NX - 1)), dma((3, 2)), dma((3, (NX - 1) * max(chunks))),
        dma((3, NZ)), dma((3, 3)), dma((3, 3)),
    ]
    outs = pl.pallas_call(
        kernel,
        out_shape=(pltpu.VMEM((n0, w), F32), pltpu.VMEM((n1, w), F32)),
        in_specs=[hbm, hbm, hbm, hbm, hbm, pl.BlockSpec(memory_space=pltpu.SMEM)],
        out_specs=(vmem, vmem),
        scratch_shapes=scratch,
        compiler_params=pltpu.CompilerParams(
            collective_id=0, has_side_effects=True, vmem_limit_bytes=60 << 20
        ),
    )(rr, rl, l0, l1, ct, rows)
    return pl.pallas_call(
        hand_over,
        out_shape=(jax.ShapeDtypeStruct((n0, w), F32), jax.ShapeDtypeStruct((n1, w), F32)),
        in_specs=[pl.BlockSpec(memory_space=pltpu.VMEM)] * 2,
        out_specs=(vmem, vmem),
        compiler_params=pltpu.CompilerParams(vmem_limit_bytes=1 << 20),
    )(*outs)


def solution(mesh):
    return jax.shard_map(
        body,
        mesh=mesh,
        in_specs=(
            P(("sub", "front"), None),
            P(("sub", "front"), None),
            P("front", "sub"),
            P("front", "sub"),
            P("front", "sub"),
            P("front", "sub"),
        ),
        out_specs=(P(("sub", "front"), None), P(("sub", "front"), None)),
        check_vma=False,
    )
```

```python
import jax
import jax.numpy as jnp
from jax import lax
from jax.experimental import pallas as pl
from jax.experimental.pallas import tpu as pltpu
from jax.sharding import PartitionSpec as P

RB = 128
NX, NZ, NY = 4, 16, 4
NF, NS = NX * NZ, NY * 2
CH = 176
F32, BF16 = jnp.float32, jnp.bfloat16


def rcopy(src, dst, ssem, rsem, dev):
    return pltpu.make_async_remote_copy(
        src_ref=src, dst_ref=dst, send_sem=ssem, recv_sem=rsem,
        device_id=dev, device_id_type=pl.DeviceIdType.MESH,
    )


def loop(n, fn):
    def step(i, carry):
        fn(i)
        return carry

    lax.fori_loop(0, n, step, 0)


def offset(k):
    half = (k + 1) // 2
    return NZ // 2 + half * (1 - 2 * (k % 2))


def kernel(
    rr_h, rl_h, l0_h, l1_h, ct_h, rows, rp_out, lp_out,
    rr, rl, l0, l0t, l1, l1t, ct, cs, cst, cols, u, wide, own, stage, part, fl,
    ag1, ag2, ag3, ub1, ub2, ub3, xr1, xr2, xr3, zs1, zs2, zs3, zr1, zr2, zr3,
    sd1, sd2, sd3, sa1, sa2, sa3, sa4, sb1, sb2, sb3, sb4,
    ld, ag_s, ag_z, ag_x, rs_s, rs_x, rs_z, sub_s, sub_r,
):
    s, f = lax.axis_index("sub"), lax.axis_index("front")
    x, z, y, c = f // NZ, f % NZ, s // 2, s % 2

    def zdev(z2):
        return (s, x * NZ + z2)

    def xdev(e):
        return (s, ((x + e) % NX) * NZ + z)

    pending = []
    barrier = pltpu.get_barrier_semaphore()

    def greet(dev):
        pl.semaphore_signal(barrier, inc=1, device_id=dev, device_id_type=pl.DeviceIdType.MESH)

    loop(NZ - 1, lambda k: greet(zdev((z + offset(k)) % NZ)))
    for e in (2, 1, 3):
        greet(xdev(e))
    for k in (2, 1, 3):
        greet((((y + k) % NY) * 2 + c, f))
    greet((s + 1 - 2 * c, f))

    loads = [
        pltpu.make_async_copy(rl_h, rl, ld.at[0]),
        pltpu.make_async_copy(l1_h, l1, ld.at[1]),
        pltpu.make_async_copy(l0_h, l0, ld.at[2]),
        pltpu.make_async_copy(rr_h, rr, ld.at[3]),
    ]
    slots = ct.shape[0]
    for j in range(slots):
        loads.append(pltpu.make_async_copy(ct_h.at[:, j * RB:(j + 1) * RB], ct.at[j], ld.at[4 + j]))
    for load in loads:
        load.start()

    n1, n0 = rl.shape[0], rr.shape[0]
    p1, p0 = ag1.shape[1], ag2.shape[1]
    blocks = l0.shape[1] // RB

    stage[...] = jnp.zeros_like(stage)
    wide[l0.shape[1]:, :] = jnp.zeros((16, wide.shape[1]), F32)
    loads[0].wait()
    stage[0:n1, :] = rl[...]
    ag1[f] = stage[0:p1, :].astype(BF16)

    def prepare():
        for load in loads[1:]:
            load.wait()
        ids = [lax.rem(rows[0, j], blocks) for j in range(slots)]
        for b in range(blocks):
            k, hit = jnp.int32(0), jnp.int32(0)
            for j in range(slots):
                same = ids[j] == b
                k = jnp.where(same, j, k)
                hit = jnp.where(same, 1, hit)
            cs[:, b * RB:(b + 1) * RB] = (ct[k].astype(F32) * hit.astype(F32)).astype(BF16)

    def pieces_of(mat, n, pad, out):
        height = mat.shape[0]

        def turn(b):
            at = pl.multiple_of(b * RB, RB)
            wide[pl.ds(at, RB), 0:height] = mat[:, pl.ds(at, RB)].T.astype(F32)

        loop(mat.shape[1] // RB, turn)
        q = 88 // n

        def cut(j):
            rows_j = wide[pl.ds(pl.multiple_of(j * 88, 8), 104), 0:height]
            for m in range(q):
                to = j * q + m
                d = (to % NZ - z + NZ) % NZ
                k = jnp.where(d < NZ // 2, NZ - 1 - 2 * d, 2 * d - NZ)
                at = pl.multiple_of((to // NZ * NZ + k) * pad, 16)
                out[pl.ds(at, pad), :] = rows_j[m * n:m * n + pad].astype(BF16)

        loop(NF // q, cut)

    prepare()
    pieces_of(l0, n0, p0, l0t)
    pl.semaphore_wait(barrier, NZ - 1 + NX - 1 + NY)

    def gather(i, buf, n, meanwhile):
        pending.append(lambda: gather_done(i, buf))
        q = 88 // n

        def slot(d):
            return x * NZ + (z + d) % NZ

        def forward(d):
            for e in (2, 1, 3):
                rcopy(buf.at[slot(d)], buf.at[slot(d)], ag_s.at[i], ag_x.at[i, e - 1], xdev(e)).start()

        def send(d, to):
            rcopy(
                buf.at[slot(d)], buf.at[slot(d)], ag_s.at[i], ag_z.at[i, (z + d) % NZ], zdev((z + to) % NZ)
            ).start()

        def arrive(d):
            d = d % NZ
            rcopy(buf.at[slot(d)], buf.at[slot(d)], ag_s.at[i], ag_z.at[i, (z + d) % NZ], zdev((z + d) % NZ)).wait_recv()

        def compact(quarter):
            def put(j):
                at = quarter * (NZ // q) + j
                pieces = [buf[at * q + m].astype(F32)[:n] for m in range(q)]
                cols[pl.ds(pl.multiple_of(at * 88, 8), 88), :] = jnp.concatenate(pieces, axis=0)

            loop(NZ // q, put)

        forward(0)
        for to in (4, 12, 3, 13, 2, 14, 1, 15):
            send(0, to)
        meanwhile()
        for d in (1, 15, 2, 14):
            arrive(d)
            forward(d)
        for way in (NZ - 4, 4):
            arrive(way)

            @pl.when(z % 2 == (way == 4))
            def _():
                send(way, NZ - way)

            for m in (3, 2, 1):
                send(way, m if way == NZ - 4 else NZ - m)
        for d in (12, 4):
            forward(d)
        for d in (3, 13):
            arrive(d)
            forward(d)
        for d in (5, 11, 6, 10, 7, 9, 8):
            arrive(d)
            forward(d)
        compact(x)
        for e in (1, 3, 2):
            quarter = (x + NX - e) % NX
            got = buf.at[pl.ds(quarter * NZ, NZ)]
            rcopy(got, got, ag_s.at[i], ag_x.at[i, e - 1], xdev(e)).wait_recv()
            compact(quarter)

    def gather_done(i, buf):
        sent = buf.at[pl.ds(0, NF - 1)]
        rcopy(sent, sent, ag_s.at[i], ag_x.at[i, 0], xdev(1)).wait_send()

    def scatter(i, pad, mat, vec, ub, xr, zs, zr):
        pending.append(lambda: scatter_done(i, ub, zs))
        g = 4

        def product(quarter, j):
            at = pl.multiple_of((quarter * NZ + j * g) * pad, 16)
            return jnp.dot(mat[pl.ds(at, g * pad), :], vec, preferred_element_type=F32)

        def xcopy(k, e):
            slot = (e - 1) * NZ + k
            return rcopy(ub.at[slot], xr.at[slot], rs_s.at[i, 0], rs_x.at[i, slot], xdev(e))

        def push(j):
            for e in (2, 1, 3):
                pieces = product((x + e) % NX, j)
                for m in range(g):
                    ub[(e - 1) * NZ + j * g + m] = pieces[m * pad:(m + 1) * pad].astype(BF16)
            for m in range(g):
                for e in (2, 1, 3):
                    xcopy(j * g + m, e).start()

        def keep(j):
            pieces = product(x, j)
            for m in range(g):
                u[j * g + m, 0:pad, :] = pieces[m * pad:(m + 1) * pad]

        def add_x(k):
            total = u[k, 0:pad, :]
            for e in (1, 3, 2):
                xcopy(k, e).wait_recv()
                total = total + xr[(e - 1) * NZ + k].astype(F32)
            return total

        def zcopy(k):
            return rcopy(zs.at[k], zr.at[k], rs_s.at[i, 1], rs_z.at[i, k], zdev((z + offset(k)) % NZ))

        def pass_on(k):
            zs[k] = add_x(k).astype(BF16)
            zcopy(k).start()

        loop(NZ // g, push)
        loop(NZ // g, keep)
        loop(NZ - 1, pass_on)
        own[0:pad, :] = add_x(NZ - 1)

        def add_z(k):
            zcopy(NZ - 2 - k).wait_recv()
            own[0:pad, :] = own[0:pad, :] + zr[NZ - 2 - k].astype(F32)

        loop(NZ - 1, add_z)

    def scatter_done(i, ub, zs):
        rcopy(ub, ub, rs_s.at[i, 0], rs_x.at[i, 0], xdev(1)).wait_send()
        rcopy(zs, zs, rs_s.at[i, 1], rs_z.at[i, 0], xdev(1)).wait_send()

    def swap(i, step, a, b):
        first = rcopy(a, b, sub_s.at[i, step], sub_r.at[i, step], (s + 1 - 2 * c, f))
        first.start()
        pending.append(first.wait_send)
        first.wait_recv()

    def sum_y(i, step, mine, d, meanwhile):
        d[y] = mine.astype(BF16)
        for k in (2, 1, 3):
            rcopy(
                d.at[y], d.at[y], sub_s.at[i, step], sub_r.at[i, step], (((y + k) % NY) * 2 + c, f)
            ).start()
        meanwhile()
        others = rcopy(
            d.at[pl.ds(0, NY - 1)], d.at[pl.ds(0, NY - 1)], sub_s.at[i, step], sub_r.at[i, step], xdev(1)
        )
        pending.append(others.wait_send)
        others.wait_recv()
        for k in range(1, NY):
            mine = mine + d[(y + k) % NY].astype(F32)
        return mine

    def sum_level(i, d, a, b, meanwhile):
        total = sum_y(i, 0, part[0:CH, :], d, meanwhile)
        a[...] = total.astype(BF16)
        swap(i, 1, a, b)
        return total + b[...].astype(F32)

    def sum_root(i, d, a, b, a2, b2, meanwhile):
        low, high = pl.multiple_of(c * CH, 8), pl.multiple_of((1 - c) * CH, 8)
        a[...] = part[pl.ds(high, CH), :].astype(BF16)
        swap(i, 0, a, b)
        total = sum_y(i, 1, part[pl.ds(low, CH), :] + b[...].astype(F32), d, meanwhile)
        a2[...] = total.astype(BF16)
        swap(i, 2, a2, b2)
        part[pl.ds(low, CH), :] = total
        part[pl.ds(high, CH), :] = b2[...].astype(F32)

    w1 = l1.shape[0]
    k1 = l1.shape[1]

    def nothing():
        pass

    gather(0, ag1, n1, nothing)
    part[0:w1, :] = jnp.dot(l1[...], cols[0:k1, :].astype(BF16), preferred_element_type=F32)
    fl[...] = sum_level(0, sd1, sa1, sb1, lambda: pieces_of(cs, n0, p0, cst))

    scatter(0, p0, cst, fl[...].astype(BF16), ub1, xr1, zs1, zr1)
    stage[0:n0, :] = rr[...] - own[0:n0, :]
    ag2[f] = stage[0:p0, :].astype(BF16)

    gather(1, ag2, n0, nothing)
    part[...] = jnp.dot(l0[...], cols[...].astype(BF16), preferred_element_type=F32)
    sum_root(1, sd2, sa2, sb2, sa4, sb4, lambda: pieces_of(l1, n1, p1, l1t))

    scatter(1, p0, l0t, part[...].astype(BF16), ub2, xr2, zs2, zr2)
    rp_out[...] = own[0:n0, :]
    ag3[f] = own[0:p0, :].astype(BF16)

    gather(2, ag3, n0, nothing)
    part[0:w1, :] = jnp.dot(cs[...], cols[...].astype(BF16), preferred_element_type=F32)
    fl[...] = fl[...] - sum_level(2, sd3, sa3, sb3, nothing)

    scatter(2, p1, l1t, fl[...].astype(BF16), ub3, xr3, zs3, zr3)
    lp_out[...] = own[0:n1, :]

    for fin in pending:
        fin()


def hand_over(a, b, c, d):
    c[...] = a[...]
    d[...] = b[...]


def body(rr, rl, l0, l1, ct, rows):
    w = rr.shape[1]
    n0, n1 = rr.shape[0], rl.shape[0]
    p0, p1 = 48, 32
    vmem = pl.BlockSpec(memory_space=pltpu.VMEM)
    hbm = pl.BlockSpec(memory_space=pl.ANY)
    slots = ct.shape[1] // RB
    scratch = [
        pltpu.VMEM(rr.shape, F32), pltpu.VMEM(rl.shape, F32),
        pltpu.VMEM(l0.shape, BF16), pltpu.VMEM((NF * p0, l0.shape[0]), BF16),
        pltpu.VMEM(l1.shape, BF16), pltpu.VMEM((NF * p1, l1.shape[0]), BF16), pltpu.VMEM((slots, ct.shape[0], RB), BF16),
        pltpu.VMEM((ct.shape[0], l0.shape[1]), BF16), pltpu.VMEM((NF * p0, ct.shape[0]), BF16),
        pltpu.VMEM((l0.shape[1], w), F32), pltpu.VMEM((NZ, p0, w), F32),
        pltpu.VMEM((l0.shape[1] + 16, l0.shape[0]), F32), pltpu.VMEM((p0, w), F32),
        pltpu.VMEM((p0, w), F32), pltpu.VMEM((l0.shape[0], w), F32), pltpu.VMEM((l1.shape[0], w), F32),
    ]
    pads = (p0, p0, p1)
    scratch += [pltpu.VMEM((NF, p, w), BF16) for p in (p1, p0, p0)]
    scratch += [pltpu.VMEM(((NX - 1) * NZ, p, w), BF16) for p in pads]
    scratch += [pltpu.VMEM(((NX - 1) * NZ, p, w), BF16) for p in pads]
    scratch += [pltpu.VMEM((NZ - 1, p, w), BF16) for p in pads]
    scratch += [pltpu.VMEM((NZ - 1, p, w), BF16) for p in pads]
    scratch += [pltpu.VMEM((NY, CH, w), BF16) for _ in range(3)]
    scratch += [pltpu.VMEM((CH, w), BF16) for _ in range(8)]
    dma = pltpu.SemaphoreType.DMA
    scratch += [
        dma((4 + slots,)), dma((3,)), dma((3, NZ)), dma((3, NX - 1)), dma((3, 2)), dma((3, (NX - 1) * NZ)),
        dma((3, NZ)), dma((3, 3)), dma((3, 3)),
    ]
    outs = pl.pallas_call(
        kernel,
        out_shape=(pltpu.VMEM((n0, w), F32), pltpu.VMEM((n1, w), F32)),
        in_specs=[hbm, hbm, hbm, hbm, hbm, pl.BlockSpec(memory_space=pltpu.SMEM)],
        out_specs=(vmem, vmem),
        scratch_shapes=scratch,
        compiler_params=pltpu.CompilerParams(
            collective_id=0, has_side_effects=True, vmem_limit_bytes=60 << 20
        ),
    )(rr, rl, l0, l1, ct, rows)
    return pl.pallas_call(
        hand_over,
        out_shape=(jax.ShapeDtypeStruct((n0, w), F32), jax.ShapeDtypeStruct((n1, w), F32)),
        in_specs=[pl.BlockSpec(memory_space=pltpu.VMEM)] * 2,
        out_specs=(vmem, vmem),
        compiler_params=pltpu.CompilerParams(vmem_limit_bytes=1 << 20),
    )(*outs)


def solution(mesh):
    return jax.shard_map(
        body,
        mesh=mesh,
        in_specs=(
            P(("sub", "front"), None),
            P(("sub", "front"), None),
            P("front", "sub"),
            P("front", "sub"),
            P("front", "sub"),
            P("front", "sub"),
        ),
        out_specs=(P(("sub", "front"), None), P(("sub", "front"), None)),
        check_vma=False,
    )
```

```python
import jax
import jax.numpy as jnp
from jax import lax
from jax.experimental import pallas as pl
from jax.experimental.pallas import tpu as pltpu
from jax.sharding import PartitionSpec as P

RB = 128
NX, NZ, NY = 4, 16, 4
NF, NS = NX * NZ, NY * 2
CH = 176
F32, BF16 = jnp.float32, jnp.bfloat16


def rcopy(src, dst, ssem, rsem, dev):
    return pltpu.make_async_remote_copy(
        src_ref=src, dst_ref=dst, send_sem=ssem, recv_sem=rsem,
        device_id=dev, device_id_type=pl.DeviceIdType.MESH,
    )


def loop(n, fn):
    def step(i, carry):
        fn(i)
        return carry

    lax.fori_loop(0, n, step, 0)


def offset(k):
    half = (k + 1) // 2
    return NZ // 2 + half * (1 - 2 * (k % 2))


def kernel(
    rr_h, rl_h, l0_h, l1_h, ct_h, rows, rp_out, lp_out,
    rr, rl, l0, l0t, l1, l1t, ct, cs, cst, cols, u, wide, own, stage, part, fl,
    ag1, ag2, ag3, ub1, ub2, ub3, xr1, xr2, xr3, zs1, zs2, zs3, zr1, zr2, zr3,
    sd1, sd2, sd3, sa1, sa2, sa3, sa4, sb1, sb2, sb3, sb4,
    ld, ag_s, ag_z, ag_x, rs_s, rs_x, rs_z, sub_s, sub_r,
):
    s, f = lax.axis_index("sub"), lax.axis_index("front")
    x, z, y, c = f // NZ, f % NZ, s // 2, s % 2

    def zdev(z2):
        return (s, x * NZ + z2)

    def xdev(e):
        return (s, ((x + e) % NX) * NZ + z)

    pending = []
    barrier = pltpu.get_barrier_semaphore()

    def greet(dev):
        pl.semaphore_signal(barrier, inc=1, device_id=dev, device_id_type=pl.DeviceIdType.MESH)

    loop(NZ - 1, lambda k: greet(zdev((z + offset(k)) % NZ)))
    for e in (2, 1, 3):
        greet(xdev(e))
    for k in (2, 1, 3):
        greet((((y + k) % NY) * 2 + c, f))
    greet((s + 1 - 2 * c, f))

    loads = [
        pltpu.make_async_copy(rl_h, rl, ld.at[0]),
        pltpu.make_async_copy(l1_h, l1, ld.at[1]),
        pltpu.make_async_copy(l0_h, l0, ld.at[2]),
        pltpu.make_async_copy(rr_h, rr, ld.at[3]),
    ]
    slots = ct.shape[0]
    for j in range(slots):
        loads.append(pltpu.make_async_copy(ct_h.at[:, j * RB:(j + 1) * RB], ct.at[j], ld.at[4 + j]))
    for load in loads:
        load.start()

    n1, n0 = rl.shape[0], rr.shape[0]
    p1, p0 = ag1.shape[1], ag2.shape[1]
    blocks = l0.shape[1] // RB

    stage[...] = jnp.zeros_like(stage)
    wide[l0.shape[1]:, :] = jnp.zeros((16, wide.shape[1]), F32)
    loads[0].wait()
    stage[0:n1, :] = rl[...]
    ag1[f] = stage[0:p1, :].astype(BF16)

    def prepare():
        for load in loads[1:]:
            load.wait()
        ids = [lax.rem(rows[0, j], blocks) for j in range(slots)]
        for b in range(blocks):
            k, hit = jnp.int32(0), jnp.int32(0)
            for j in range(slots):
                same = ids[j] == b
                k = jnp.where(same, j, k)
                hit = jnp.where(same, 1, hit)
            cs[:, b * RB:(b + 1) * RB] = (ct[k].astype(F32) * hit.astype(F32)).astype(BF16)

    def pieces_of(mat, n, pad, out):
        height = mat.shape[0]

        def turn(b):
            at = pl.multiple_of(b * RB, RB)
            wide[pl.ds(at, RB), 0:height] = mat[:, pl.ds(at, RB)].T.astype(F32)

        loop(mat.shape[1] // RB, turn)
        q = 88 // n

        def cut(j):
            rows_j = wide[pl.ds(pl.multiple_of(j * 88, 8), 104), 0:height]
            for m in range(q):
                to = j * q + m
                d = (to % NZ - z + NZ) % NZ
                k = jnp.where(d < NZ // 2, NZ - 1 - 2 * d, 2 * d - NZ)
                at = pl.multiple_of((to // NZ * NZ + k) * pad, 16)
                out[pl.ds(at, pad), :] = rows_j[m * n:m * n + pad].astype(BF16)

        loop(NF // q, cut)

    prepare()
    pieces_of(l0, n0, p0, l0t)
    pl.semaphore_wait(barrier, NZ - 1 + NX - 1 + NY)

    def gather(i, buf, n, meanwhile):
        pending.append(lambda: gather_done(i, buf))
        q = 88 // n

        def slot(d):
            return x * NZ + (z + d) % NZ

        def forward(d):
            for e in (2, 1, 3):
                rcopy(buf.at[slot(d)], buf.at[slot(d)], ag_s.at[i], ag_x.at[e - 1], xdev(e)).start()

        def send(d, to):
            rcopy(
                buf.at[slot(d)], buf.at[slot(d)], ag_s.at[i], ag_z.at[(z + d) % NZ], zdev((z + to) % NZ)
            ).start()

        def arrive(d):
            d = d % NZ
            rcopy(buf.at[slot(d)], buf.at[slot(d)], ag_s.at[i], ag_z.at[(z + d) % NZ], zdev((z + d) % NZ)).wait_recv()

        def compact(quarter):
            def put(j):
                at = quarter * (NZ // q) + j
                pieces = [buf[at * q + m].astype(F32)[:n] for m in range(q)]
                cols[pl.ds(pl.multiple_of(at * 88, 8), 88), :] = jnp.concatenate(pieces, axis=0)

            loop(NZ // q, put)

        forward(0)
        for to in (4, 12, 3, 13, 2, 14, 1, 15):
            send(0, to)
        meanwhile()
        for d in (1, 15, 2, 14):
            arrive(d)
            forward(d)
        for way in (NZ - 4, 4):
            arrive(way)

            @pl.when(z % 2 == (way == 4))
            def _():
                send(way, NZ - way)

            for m in (3, 2, 1):
                send(way, m if way == NZ - 4 else NZ - m)
        for d in (12, 4):
            forward(d)
        for d in (3, 13):
            arrive(d)
            forward(d)
        for d in (5, 11, 6, 10, 7, 9, 8):
            arrive(d)
            forward(d)
        compact(x)
        for e in (1, 3, 2):
            quarter = (x + NX - e) % NX
            got = buf.at[pl.ds(quarter * NZ, NZ)]
            rcopy(got, got, ag_s.at[i], ag_x.at[e - 1], xdev(e)).wait_recv()
            compact(quarter)

    def gather_done(i, buf):
        sent = buf.at[pl.ds(0, NF - 1)]
        rcopy(sent, sent, ag_s.at[i], ag_x.at[0], xdev(1)).wait_send()

    def scatter(i, pad, mat, vec, ub, xr, zs, zr):
        pending.append(lambda: scatter_done(i, ub, zs))
        g = 4

        def product(quarter, j):
            at = pl.multiple_of((quarter * NZ + j * g) * pad, 16)
            return jnp.dot(mat[pl.ds(at, g * pad), :], vec, preferred_element_type=F32)

        def xcopy(k, e):
            slot = k * (NX - 1) + e - 1
            return rcopy(ub.at[slot], xr.at[slot], rs_s.at[i, 0], rs_x.at[k], xdev(e))

        def push(j):
            for e in (2, 1, 3):
                pieces = product((x + e) % NX, j)
                for m in range(g):
                    ub[(j * g + m) * (NX - 1) + e - 1] = pieces[m * pad:(m + 1) * pad].astype(BF16)
            for m in range(g):
                for e in (2, 1, 3):
                    xcopy(j * g + m, e).start()

        def keep(j):
            pieces = product(x, j)
            for m in range(g):
                u[j * g + m, 0:pad, :] = pieces[m * pad:(m + 1) * pad]

        def add_x(k):
            total = u[k, 0:pad, :]
            got = xr.at[pl.ds(k * (NX - 1), NX - 1)]
            rcopy(got, got, rs_s.at[i, 0], rs_x.at[k], xdev(1)).wait_recv()
            for e in (1, 3, 2):
                total = total + xr[k * (NX - 1) + e - 1].astype(F32)
            return total

        def zcopy(k):
            return rcopy(zs.at[k], zr.at[k], rs_s.at[i, 1], rs_z.at[k], zdev((z + offset(k)) % NZ))

        def pass_on(k):
            zs[k] = add_x(k).astype(BF16)
            zcopy(k).start()

        loop(NZ // g, push)
        loop(NZ // g, keep)
        loop(NZ - 1, pass_on)
        own[0:pad, :] = add_x(NZ - 1)

        def add_z(k):
            zcopy(NZ - 2 - k).wait_recv()
            own[0:pad, :] = own[0:pad, :] + zr[NZ - 2 - k].astype(F32)

        loop(NZ - 1, add_z)

    def scatter_done(i, ub, zs):
        rcopy(ub, ub, rs_s.at[i, 0], rs_x.at[0], xdev(1)).wait_send()
        rcopy(zs, zs, rs_s.at[i, 1], rs_z.at[0], xdev(1)).wait_send()

    def swap(i, step, a, b):
        first = rcopy(a, b, sub_s.at[i, step], sub_r.at[i, step], (s + 1 - 2 * c, f))
        first.start()
        pending.append(first.wait_send)
        first.wait_recv()

    def sum_y(i, step, mine, d, meanwhile):
        d[y] = mine.astype(BF16)
        for k in (2, 1, 3):
            rcopy(
                d.at[y], d.at[y], sub_s.at[i, step], sub_r.at[i, step], (((y + k) % NY) * 2 + c, f)
            ).start()
        meanwhile()
        others = rcopy(
            d.at[pl.ds(0, NY - 1)], d.at[pl.ds(0, NY - 1)], sub_s.at[i, step], sub_r.at[i, step], xdev(1)
        )
        pending.append(others.wait_send)
        others.wait_recv()
        for k in range(1, NY):
            mine = mine + d[(y + k) % NY].astype(F32)
        return mine

    def sum_level(i, d, a, b, meanwhile):
        total = sum_y(i, 0, part[0:CH, :], d, meanwhile)
        a[...] = total.astype(BF16)
        swap(i, 1, a, b)
        return total + b[...].astype(F32)

    def sum_root(i, d, a, b, a2, b2, meanwhile):
        low, high = pl.multiple_of(c * CH, 8), pl.multiple_of((1 - c) * CH, 8)
        a[...] = part[pl.ds(high, CH), :].astype(BF16)
        swap(i, 0, a, b)
        total = sum_y(i, 1, part[pl.ds(low, CH), :] + b[...].astype(F32), d, meanwhile)
        a2[...] = total.astype(BF16)
        swap(i, 2, a2, b2)
        part[pl.ds(low, CH), :] = total
        part[pl.ds(high, CH), :] = b2[...].astype(F32)

    w1 = l1.shape[0]
    k1 = l1.shape[1]

    def nothing():
        pass

    gather(0, ag1, n1, nothing)
    part[0:w1, :] = jnp.dot(l1[...], cols[0:k1, :].astype(BF16), preferred_element_type=F32)
    fl[...] = sum_level(0, sd1, sa1, sb1, lambda: pieces_of(cs, n0, p0, cst))

    scatter(0, p0, cst, fl[...].astype(BF16), ub1, xr1, zs1, zr1)
    stage[0:n0, :] = rr[...] - own[0:n0, :]
    ag2[f] = stage[0:p0, :].astype(BF16)

    gather(1, ag2, n0, nothing)
    part[...] = jnp.dot(l0[...], cols[...].astype(BF16), preferred_element_type=F32)
    sum_root(1, sd2, sa2, sb2, sa4, sb4, lambda: pieces_of(l1, n1, p1, l1t))

    scatter(1, p0, l0t, part[...].astype(BF16), ub2, xr2, zs2, zr2)
    rp_out[...] = own[0:n0, :]
    ag3[f] = own[0:p0, :].astype(BF16)

    gather(2, ag3, n0, nothing)
    part[0:w1, :] = jnp.dot(cs[...], cols[...].astype(BF16), preferred_element_type=F32)
    fl[...] = fl[...] - sum_level(2, sd3, sa3, sb3, nothing)

    scatter(2, p1, l1t, fl[...].astype(BF16), ub3, xr3, zs3, zr3)
    lp_out[...] = own[0:n1, :]

    for fin in pending:
        fin()


def hand_over(a, b, c, d):
    c[...] = a[...]
    d[...] = b[...]


def body(rr, rl, l0, l1, ct, rows):
    w = rr.shape[1]
    n0, n1 = rr.shape[0], rl.shape[0]
    p0, p1 = 48, 32
    vmem = pl.BlockSpec(memory_space=pltpu.VMEM)
    hbm = pl.BlockSpec(memory_space=pl.ANY)
    slots = ct.shape[1] // RB
    scratch = [
        pltpu.VMEM(rr.shape, F32), pltpu.VMEM(rl.shape, F32),
        pltpu.VMEM(l0.shape, BF16), pltpu.VMEM((NF * p0, l0.shape[0]), BF16),
        pltpu.VMEM(l1.shape, BF16), pltpu.VMEM((NF * p1, l1.shape[0]), BF16), pltpu.VMEM((slots, ct.shape[0], RB), BF16),
        pltpu.VMEM((ct.shape[0], l0.shape[1]), BF16), pltpu.VMEM((NF * p0, ct.shape[0]), BF16),
        pltpu.VMEM((l0.shape[1], w), F32), pltpu.VMEM((NZ, p0, w), F32),
        pltpu.VMEM((l0.shape[1] + 16, l0.shape[0]), F32), pltpu.VMEM((p0, w), F32),
        pltpu.VMEM((p0, w), F32), pltpu.VMEM((l0.shape[0], w), F32), pltpu.VMEM((l1.shape[0], w), F32),
    ]
    pads = (p0, p0, p1)
    scratch += [pltpu.VMEM((NF, p, w), BF16) for p in (p1, p0, p0)]
    scratch += [pltpu.VMEM(((NX - 1) * NZ, p, w), BF16) for p in pads]
    scratch += [pltpu.VMEM(((NX - 1) * NZ, p, w), BF16) for p in pads]
    scratch += [pltpu.VMEM((NZ - 1, p, w), BF16) for p in pads]
    scratch += [pltpu.VMEM((NZ - 1, p, w), BF16) for p in pads]
    scratch += [pltpu.VMEM((NY, CH, w), BF16) for _ in range(3)]
    scratch += [pltpu.VMEM((CH, w), BF16) for _ in range(8)]
    dma = pltpu.SemaphoreType.DMA
    scratch += [
        dma((4 + slots,)), dma((3,)), dma((NZ,)), dma((NX - 1,)), dma((3, 2)), dma((NZ,)),
        dma((NZ,)), dma((3, 3)), dma((3, 3)),
    ]
    outs = pl.pallas_call(
        kernel,
        out_shape=(pltpu.VMEM((n0, w), F32), pltpu.VMEM((n1, w), F32)),
        in_specs=[hbm, hbm, hbm, hbm, hbm, pl.BlockSpec(memory_space=pltpu.SMEM)],
        out_specs=(vmem, vmem),
        scratch_shapes=scratch,
        compiler_params=pltpu.CompilerParams(
            collective_id=0, has_side_effects=True, vmem_limit_bytes=60 << 20
        ),
    )(rr, rl, l0, l1, ct, rows)
    return pl.pallas_call(
        hand_over,
        out_shape=(jax.ShapeDtypeStruct((n0, w), F32), jax.ShapeDtypeStruct((n1, w), F32)),
        in_specs=[pl.BlockSpec(memory_space=pltpu.VMEM)] * 2,
        out_specs=(vmem, vmem),
        compiler_params=pltpu.CompilerParams(vmem_limit_bytes=1 << 20),
    )(*outs)


def solution(mesh):
    return jax.shard_map(
        body,
        mesh=mesh,
        in_specs=(
            P(("sub", "front"), None),
            P(("sub", "front"), None),
            P("front", "sub"),
            P("front", "sub"),
            P("front", "sub"),
            P("front", "sub"),
        ),
        out_specs=(P(("sub", "front"), None), P(("sub", "front"), None)),
        check_vma=False,
    )
```

```python
import jax
import jax.numpy as jnp
from jax import lax
from jax.experimental import pallas as pl
from jax.experimental.pallas import tpu as pltpu
from jax.sharding import PartitionSpec as P

RB = 128
NX, NZ, NY = 4, 16, 4
NF, NS = NX * NZ, NY * 2
CH = 176
F32, BF16 = jnp.float32, jnp.bfloat16


def rcopy(src, dst, ssem, rsem, dev):
    return pltpu.make_async_remote_copy(
        src_ref=src, dst_ref=dst, send_sem=ssem, recv_sem=rsem,
        device_id=dev, device_id_type=pl.DeviceIdType.MESH,
    )


def loop(n, fn):
    def step(i, carry):
        fn(i)
        return carry

    lax.fori_loop(0, n, step, 0)


def offset(k):
    half = (k + 1) // 2
    return NZ // 2 + half * (1 - 2 * (k % 2))


def kernel(
    rr_h, rl_h, l0_h, l1_h, ct_h, rows, rp_out, lp_out,
    rr, rl, l0, l0t, l1, l1t, ct, cs, cst, cols, u, wide, own, stage, part, fl,
    ag1, ag2, ag3, ub1, ub2, ub3, xr1, xr2, xr3, zs1, zs2, zs3, zr1, zr2, zr3,
    sd1, sd2, sd3, sa1, sa2, sa3, sa4, sb1, sb2, sb3, sb4,
    ld, ag_s, ag_z, ag_x, rs_s, rs_x, rs_z, sub_s, sub_r,
):
    s, f = lax.axis_index("sub"), lax.axis_index("front")
    x, z, y, c = f // NZ, f % NZ, s // 2, s % 2

    def zdev(z2):
        return (s, x * NZ + z2)

    def xdev(e):
        return (s, ((x + e) % NX) * NZ + z)

    pending = []
    barrier = pltpu.get_barrier_semaphore()

    def greet(dev):
        pl.semaphore_signal(barrier, inc=1, device_id=dev, device_id_type=pl.DeviceIdType.MESH)

    loop(NZ - 1, lambda k: greet(zdev((z + offset(k)) % NZ)))
    for e in (2, 1, 3):
        greet(xdev(e))
    for k in (2, 1, 3):
        greet((((y + k) % NY) * 2 + c, f))
    greet((s + 1 - 2 * c, f))

    loads = [
        pltpu.make_async_copy(rl_h, rl, ld.at[0]),
        pltpu.make_async_copy(l1_h, l1, ld.at[1]),
        pltpu.make_async_copy(l0_h, l0, ld.at[2]),
        pltpu.make_async_copy(rr_h, rr, ld.at[3]),
    ]
    slots = ct.shape[0]
    for j in range(slots):
        loads.append(pltpu.make_async_copy(ct_h.at[:, j * RB:(j + 1) * RB], ct.at[j], ld.at[4]))
    for load in loads:
        load.start()

    n1, n0 = rl.shape[0], rr.shape[0]
    p1, p0 = ag1.shape[1], ag2.shape[1]
    blocks = l0.shape[1] // RB

    stage[...] = jnp.zeros_like(stage)
    wide[l0.shape[1]:, :] = jnp.zeros((16, wide.shape[1]), F32)
    loads[0].wait()
    stage[0:n1, :] = rl[...]
    ag1[f] = stage[0:p1, :].astype(BF16)

    def prepare():
        for load in loads[1:4]:
            load.wait()
        pltpu.make_async_copy(ct, ct, ld.at[4]).wait()
        ids = [lax.rem(rows[0, j], blocks) for j in range(slots)]
        for b in range(blocks):
            k, hit = jnp.int32(0), jnp.int32(0)
            for j in range(slots):
                same = ids[j] == b
                k = jnp.where(same, j, k)
                hit = jnp.where(same, 1, hit)
            cs[:, b * RB:(b + 1) * RB] = (ct[k].astype(F32) * hit.astype(F32)).astype(BF16)

    def pieces_of(mat, n, pad, out):
        height = mat.shape[0]

        def turn(b):
            at = pl.multiple_of(b * RB, RB)
            wide[pl.ds(at, RB), 0:height] = mat[:, pl.ds(at, RB)].T.astype(F32)

        loop(mat.shape[1] // RB, turn)
        q = 88 // n

        def cut(j):
            rows_j = wide[pl.ds(pl.multiple_of(j * 88, 8), 104), 0:height]
            for m in range(q):
                to = j * q + m
                d = (to % NZ - z + NZ) % NZ
                k = jnp.where(d < NZ // 2, NZ - 1 - 2 * d, 2 * d - NZ)
                at = pl.multiple_of((to // NZ * NZ + k) * pad, 16)
                out[pl.ds(at, pad), :] = rows_j[m * n:m * n + pad].astype(BF16)

        loop(NF // q, cut)

    prepare()
    pieces_of(l0, n0, p0, l0t)
    pl.semaphore_wait(barrier, NZ - 1 + NX - 1 + NY)

    def gather(i, buf, n, meanwhile):
        pending.append(lambda: gather_done(i, buf))
        q = 88 // n

        def slot(d):
            return x * NZ + (z + d) % NZ

        def forward(d):
            for e in (2, 1, 3):
                rcopy(buf.at[slot(d)], buf.at[slot(d)], ag_s.at[i], ag_x.at[e - 1], xdev(e)).start()

        def send(d, to):
            rcopy(
                buf.at[slot(d)], buf.at[slot(d)], ag_s.at[i], ag_z.at[(z + d) % NZ], zdev((z + to) % NZ)
            ).start()

        def arrive(d):
            d = d % NZ
            rcopy(buf.at[slot(d)], buf.at[slot(d)], ag_s.at[i], ag_z.at[(z + d) % NZ], zdev((z + d) % NZ)).wait_recv()

        def compact(quarter):
            def put(j):
                at = quarter * (NZ // q) + j
                pieces = [buf[at * q + m].astype(F32)[:n] for m in range(q)]
                cols[pl.ds(pl.multiple_of(at * 88, 8), 88), :] = jnp.concatenate(pieces, axis=0)

            loop(NZ // q, put)

        forward(0)
        for to in (4, 12, 3, 13, 2, 14, 1, 15):
            send(0, to)
        meanwhile()
        for d in (1, 15, 2, 14):
            arrive(d)
            forward(d)
        for way in (NZ - 4, 4):
            arrive(way)

            @pl.when(z % 2 == (way == 4))
            def _():
                send(way, NZ - way)

            for m in (3, 2, 1):
                send(way, m if way == NZ - 4 else NZ - m)
        for d in (12, 4):
            forward(d)
        for d in (3, 13):
            arrive(d)
            forward(d)
        for d in (5, 11, 6, 10, 7, 9, 8):
            arrive(d)
            forward(d)
        compact(x)
        for e in (1, 3, 2):
            quarter = (x + NX - e) % NX
            got = buf.at[pl.ds(quarter * NZ, NZ)]
            rcopy(got, got, ag_s.at[i], ag_x.at[e - 1], xdev(e)).wait_recv()
            compact(quarter)

    def gather_done(i, buf):
        sent = buf.at[pl.ds(0, NF - 1)]
        rcopy(sent, sent, ag_s.at[i], ag_x.at[0], xdev(1)).wait_send()

    def scatter(i, pad, mat, vec, ub, xr, zs, zr):
        pending.append(lambda: scatter_done(i, ub, zs))
        g = 4

        def product(quarter, j):
            at = pl.multiple_of((quarter * NZ + j * g) * pad, 16)
            return jnp.dot(mat[pl.ds(at, g * pad), :], vec, preferred_element_type=F32)

        def xcopy(k, e):
            slot = k * (NX - 1) + e - 1
            return rcopy(ub.at[slot], xr.at[slot], rs_s.at[i, 0], rs_x.at[k], xdev(e))

        def push(j):
            for e in (2, 1, 3):
                pieces = product((x + e) % NX, j)
                for m in range(g):
                    ub[(j * g + m) * (NX - 1) + e - 1] = pieces[m * pad:(m + 1) * pad].astype(BF16)
            for m in range(g):
                for e in (2, 1, 3):
                    xcopy(j * g + m, e).start()

        def keep(j):
            pieces = product(x, j)
            for m in range(g):
                u[j * g + m, 0:pad, :] = pieces[m * pad:(m + 1) * pad]

        def add_x(k):
            total = u[k, 0:pad, :]
            got = xr.at[pl.ds(k * (NX - 1), NX - 1)]
            rcopy(got, got, rs_s.at[i, 0], rs_x.at[k], xdev(1)).wait_recv()
            for e in (1, 3, 2):
                total = total + xr[k * (NX - 1) + e - 1].astype(F32)
            return total

        def zcopy(k):
            return rcopy(zs.at[k], zr.at[k], rs_s.at[i, 1], rs_z.at[k], zdev((z + offset(k)) % NZ))

        def pass_on(k):
            zs[k] = add_x(k).astype(BF16)
            zcopy(k).start()

        loop(NZ // g, push)
        loop(NZ // g, keep)
        loop(NZ - 1, pass_on)
        own[0:pad, :] = add_x(NZ - 1)

        def add_z(k):
            zcopy(NZ - 2 - k).wait_recv()
            own[0:pad, :] = own[0:pad, :] + zr[NZ - 2 - k].astype(F32)

        loop(NZ - 1, add_z)

    def scatter_done(i, ub, zs):
        rcopy(ub, ub, rs_s.at[i, 0], rs_x.at[0], xdev(1)).wait_send()
        rcopy(zs, zs, rs_s.at[i, 1], rs_z.at[0], xdev(1)).wait_send()

    def swap(i, step, a, b):
        first = rcopy(a, b, sub_s.at[i, step], sub_r.at[i, step], (s + 1 - 2 * c, f))
        first.start()
        pending.append(first.wait_send)
        first.wait_recv()

    def sum_y(i, step, mine, d, meanwhile):
        d[y] = mine.astype(BF16)
        for k in (2, 1, 3):
            rcopy(
                d.at[y], d.at[y], sub_s.at[i, step], sub_r.at[i, step], (((y + k) % NY) * 2 + c, f)
            ).start()
        meanwhile()
        others = rcopy(
            d.at[pl.ds(0, NY - 1)], d.at[pl.ds(0, NY - 1)], sub_s.at[i, step], sub_r.at[i, step], xdev(1)
        )
        pending.append(others.wait_send)
        others.wait_recv()
        for k in range(1, NY):
            mine = mine + d[(y + k) % NY].astype(F32)
        return mine

    def sum_level(i, d, a, b, meanwhile):
        total = sum_y(i, 0, part[0:CH, :], d, meanwhile)
        a[...] = total.astype(BF16)
        swap(i, 1, a, b)
        return total + b[...].astype(F32)

    def sum_root(i, d, a, b, a2, b2, meanwhile):
        low, high = pl.multiple_of(c * CH, 8), pl.multiple_of((1 - c) * CH, 8)
        a[...] = part[pl.ds(high, CH), :].astype(BF16)
        swap(i, 0, a, b)
        total = sum_y(i, 1, part[pl.ds(low, CH), :] + b[...].astype(F32), d, meanwhile)
        a2[...] = total.astype(BF16)
        swap(i, 2, a2, b2)
        part[pl.ds(low, CH), :] = total
        part[pl.ds(high, CH), :] = b2[...].astype(F32)

    w1 = l1.shape[0]
    k1 = l1.shape[1]

    def nothing():
        pass

    gather(0, ag1, n1, nothing)
    part[0:w1, :] = jnp.dot(l1[...], cols[0:k1, :].astype(BF16), preferred_element_type=F32)
    fl[...] = sum_level(0, sd1, sa1, sb1, lambda: pieces_of(cs, n0, p0, cst))

    scatter(0, p0, cst, fl[...].astype(BF16), ub1, xr1, zs1, zr1)
    stage[0:n0, :] = rr[...] - own[0:n0, :]
    ag2[f] = stage[0:p0, :].astype(BF16)

    gather(1, ag2, n0, nothing)
    part[...] = jnp.dot(l0[...], cols[...].astype(BF16), preferred_element_type=F32)
    sum_root(1, sd2, sa2, sb2, sa4, sb4, lambda: pieces_of(l1, n1, p1, l1t))

    scatter(1, p0, l0t, part[...].astype(BF16), ub2, xr2, zs2, zr2)
    rp_out[...] = own[0:n0, :]
    ag3[f] = own[0:p0, :].astype(BF16)

    gather(2, ag3, n0, nothing)
    part[0:w1, :] = jnp.dot(cs[...], cols[...].astype(BF16), preferred_element_type=F32)
    fl[...] = fl[...] - sum_level(2, sd3, sa3, sb3, nothing)

    scatter(2, p1, l1t, fl[...].astype(BF16), ub3, xr3, zs3, zr3)
    lp_out[...] = own[0:n1, :]

    for fin in pending:
        fin()


def hand_over(a, b, c, d):
    c[...] = a[...]
    d[...] = b[...]


def body(rr, rl, l0, l1, ct, rows):
    w = rr.shape[1]
    n0, n1 = rr.shape[0], rl.shape[0]
    p0, p1 = 48, 32
    vmem = pl.BlockSpec(memory_space=pltpu.VMEM)
    hbm = pl.BlockSpec(memory_space=pl.ANY)
    slots = ct.shape[1] // RB
    scratch = [
        pltpu.VMEM(rr.shape, F32), pltpu.VMEM(rl.shape, F32),
        pltpu.VMEM(l0.shape, BF16), pltpu.VMEM((NF * p0, l0.shape[0]), BF16),
        pltpu.VMEM(l1.shape, BF16), pltpu.VMEM((NF * p1, l1.shape[0]), BF16), pltpu.VMEM((slots, ct.shape[0], RB), BF16),
        pltpu.VMEM((ct.shape[0], l0.shape[1]), BF16), pltpu.VMEM((NF * p0, ct.shape[0]), BF16),
        pltpu.VMEM((l0.shape[1], w), F32), pltpu.VMEM((NZ, p0, w), F32),
        pltpu.VMEM((l0.shape[1] + 16, l0.shape[0]), F32), pltpu.VMEM((p0, w), F32),
        pltpu.VMEM((p0, w), F32), pltpu.VMEM((l0.shape[0], w), F32), pltpu.VMEM((l1.shape[0], w), F32),
    ]
    pads = (p0, p0, p1)
    scratch += [pltpu.VMEM((NF, p, w), BF16) for p in (p1, p0, p0)]
    scratch += [pltpu.VMEM(((NX - 1) * NZ, p, w), BF16) for p in pads]
    scratch += [pltpu.VMEM(((NX - 1) * NZ, p, w), BF16) for p in pads]
    scratch += [pltpu.VMEM((NZ - 1, p, w), BF16) for p in pads]
    scratch += [pltpu.VMEM((NZ - 1, p, w), BF16) for p in pads]
    scratch += [pltpu.VMEM((NY, CH, w), BF16) for _ in range(3)]
    scratch += [pltpu.VMEM((CH, w), BF16) for _ in range(8)]
    dma = pltpu.SemaphoreType.DMA
    scratch += [
        dma((5,)), dma((3,)), dma((NZ,)), dma((NX - 1,)), dma((3, 2)), dma((NZ,)),
        dma((NZ,)), dma((3, 3)), dma((3, 3)),
    ]
    outs = pl.pallas_call(
        kernel,
        out_shape=(pltpu.VMEM((n0, w), F32), pltpu.VMEM((n1, w), F32)),
        in_specs=[hbm, hbm, hbm, hbm, hbm, pl.BlockSpec(memory_space=pltpu.SMEM)],
        out_specs=(vmem, vmem),
        scratch_shapes=scratch,
        compiler_params=pltpu.CompilerParams(
            collective_id=0, has_side_effects=True, vmem_limit_bytes=60 << 20
        ),
    )(rr, rl, l0, l1, ct, rows)
    return pl.pallas_call(
        hand_over,
        out_shape=(jax.ShapeDtypeStruct((n0, w), F32), jax.ShapeDtypeStruct((n1, w), F32)),
        in_specs=[pl.BlockSpec(memory_space=pltpu.VMEM)] * 2,
        out_specs=(vmem, vmem),
        compiler_params=pltpu.CompilerParams(vmem_limit_bytes=1 << 20),
    )(*outs)


def solution(mesh):
    return jax.shard_map(
        body,
        mesh=mesh,
        in_specs=(
            P(("sub", "front"), None),
            P(("sub", "front"), None),
            P("front", "sub"),
            P("front", "sub"),
            P("front", "sub"),
            P("front", "sub"),
        ),
        out_specs=(P(("sub", "front"), None), P(("sub", "front"), None)),
        check_vma=False,
    )
```
